128 devices in a mesh: dp: 8 (over x, core), help: 16 (over y, z).
Axes of the slice: x: 4, y: 4, z: 4, core: 2. Of those that a mesh axis runs over, the one named last changes fastest.
Arguments:
- coeffs: bfloat16 [8, 1024, 9, 256], P('dp', 'help'), may hold values from -6 to 6
- cotangent: bfloat16 [8, 1024, 9, 256], P('dp', 'help'), may hold values from -6 to 6
- w_zero: bfloat16 [768, 768], replicated, may hold values from -0.21875 to 0.21875
- w_one: bfloat16 [2, 512, 512], replicated, may hold values from -0.25 to 0.25
- w_two: bfloat16 [2, 256, 256], replicated, may hold values from -0.375 to 0.375
- source: int32 [8, 16384], P('dp', 'help'), may hold values from 0 to 191, as said below
- target: int32 [8, 16384], P('dp', 'help'), may hold values from 0 to 63
- rotation: bfloat16 [8, 35, 16384], P('dp', None, 'help'), may hold values from -3 to 3
- gate: bfloat16 [8, 16384], P('dp', 'help'), may hold values from 0.099609375 to 0.5
- tile_live: int32 [8, 256], P('dp', 'help'), may hold values from 0 to 1, as said below
Outputs:
- updated: bfloat16 [8, 1024, 9, 256], P('dp', 'help')
- grad_coeffs: bfloat16 [8, 1024, 9, 256], P('dp', 'help')
- grad_w_zero: float32 [768, 768], replicated
- grad_w_one: float32 [2, 512, 512], replicated
- grad_w_two: float32 [2, 256, 256], replicated
The draws below stay inside these ranges and needn't reach their ends.
Inputs may be any that keep to these rules, and one draw needn't show every extreme that they name: `source`: indices 0 to 63 name the block of the device before along help, then its own block, then the block after; the first device along help never names the block before it, the last never the block after it. `tile_live`: on each device its live tiles come first; each device has two or more live tiles, and in every system one device has all 16 live.
All inputs are finite; a program needn't handle non-finite values.
Results may differ from the reference program's by a relative error of at most 0.0052.
Values may be sent and summed in bfloat16 or wider, within the bound.
A program may use at most 192 MiB of HBM per device.

```python
import math
from functools import reduce
import jax
import jax.numpy as jnp
from jax import lax

C = 256
COEF = 9
ROT = 35
TILE = 64
A_DEV = 64
TILES_DEV = 16
SYSTEMS = 8
ATOMS = 1024
EDGES_DEV = 1024
EDGES = 16384


def draw_source(key, part):
    key = jax.random.fold_in(key, 11)
    helpers = ATOMS // A_DEV
    owner = (jnp.arange(EDGES, dtype=jnp.int32) // EDGES_DEV)[None, :]
    lowest = jnp.where(owner == 0, A_DEV, 0)
    highest = jnp.where(owner == helpers - 1, 2 * A_DEV, 3 * A_DEV)
    raw_pick = jax.random.randint(key, (SYSTEMS, EDGES), 0, 3 * A_DEV)
    return (lowest + raw_pick % (highest - lowest)).astype(jnp.int32)


def draw_tile_live(key, part):
    key = jax.random.fold_in(key, 23)
    helpers = ATOMS // A_DEV
    first_key, second_key = jax.random.split(key)
    counts = jax.random.randint(first_key, (SYSTEMS, helpers), 2, max(3, TILES_DEV // 2 + 1))
    busiest = jax.random.randint(second_key, (SYSTEMS, 1), 0, helpers)
    counts = jnp.where(jnp.arange(helpers, dtype=jnp.int32)[None, :] == busiest, TILES_DEV, counts)
    places = jnp.arange(TILES_DEV, dtype=jnp.int32)
    flags = (places[None, None, :] < counts[:, :, None]).astype(jnp.int32)
    return flags.reshape(SYSTEMS, helpers * TILES_DEV)


def with_ends(values, rng, low, largest):
    longest = values.shape.index(max(values.shape))
    spots = []
    for shift in (0, 1):
        where = [jax.random.randint(jax.random.fold_in(rng, axis), (), 0, length) for axis, length in enumerate(values.shape)]
        where[longest] = (where[longest] + shift) % values.shape[longest]
        spots.append(tuple(where))
    return values.at[spots[0]].set(low).at[spots[1]].set(largest)


def levels(rng, shape, cuts, smallest, high):
    level, own = 1.0, jax.random.fold_in(rng, 6)
    for position, parts in cuts:
        steps = jnp.exp(jax.random.uniform(jax.random.fold_in(own, position), (parts,), jnp.float32, smallest / len(cuts), high / len(cuts)))
        level = level * jnp.repeat(steps, shape[position] // parts).reshape([-1 if axis == position else 1 for axis in range(len(shape))])
    return level


def gaussian(stream_key, shape, spread, bound, shards=(), kind=jnp.bfloat16):
    level = levels(stream_key, shape, shards, -0.22, 0.18) if shards else 1.0
    array = jax.random.normal(stream_key, shape, jnp.float32) * spread * level
    return jnp.minimum(jnp.maximum(array, -bound), bound).astype(kind)


def setup_inputs(seed: int = 0) -> dict:
    key_of = jax.random.split(jax.random.key(seed), 11)
    coeffs = gaussian(key_of[0], (SYSTEMS, ATOMS, COEF, C), 1.0, 6.0, ((0, 8), (1, 16)))
    cotangent = gaussian(key_of[1], (SYSTEMS, ATOMS, COEF, C), 1.0, 6.0, ((0, 8), (1, 16)))
    w_zero = gaussian(key_of[2], (3 * C, 3 * C), (3 * C) ** -0.5, 0.21875)
    w_one = gaussian(key_of[3], (2, 2 * C, 2 * C), (2 * C) ** -0.5, 0.25)
    w_two = gaussian(key_of[4], (2, C, C), C ** -0.5, 0.375)
    source = draw_source(jax.random.fold_in(key_of[10], 71), 0)
    target = with_ends(jax.random.randint(key_of[6], (SYSTEMS, EDGES), 0, A_DEV), jax.random.fold_in(key_of[6], 1), 0, A_DEV - 1).astype(jnp.int32)
    rotation = gaussian(key_of[7], (SYSTEMS, ROT, EDGES), 0.5, 3.0, ((0, 8), (2, 16)))
    gate = jnp.clip(jnp.exp(math.log(0.5) - 1.6133518 * jax.random.uniform(key_of[8], (SYSTEMS, EDGES), jnp.float32) ** levels(key_of[8], (SYSTEMS, EDGES), ((0, 8), (1, 16)), -0.2, 0.2)), 0.099609375, 0.5).astype(jnp.bfloat16)
    tile_live = draw_tile_live(jax.random.fold_in(key_of[10], 71), 0)
    return dict(coeffs=coeffs, cotangent=cotangent, w_zero=w_zero, w_one=w_one, w_two=w_two, source=source, target=target, rotation=rotation, gate=gate, tile_live=tile_live)


rotation_blocks = ((0, 1, 0), (1, 3, 1), (10, 5, 4))


def rotate(rotations, row_data, inverse):
    pieces = []
    for offset, extent, first_coef in rotation_blocks:
        for row_k in range(extent):
            products = []
            for col_j in range(extent):
                entry_index = offset + (col_j * extent + row_k if inverse else row_k * extent + col_j)
                products.append(rotations[:, entry_index][:, None] * row_data[:, first_coef + col_j].astype(jnp.float32))
            pieces.append(reduce(jnp.add, products))
    return jnp.stack(pieces, axis=1)


def plain_dot(left, weight):
    return jnp.dot(left, weight, preferred_element_type=jnp.float32)


def transposed_dot(left, right):
    return lax.dot_general(left, right, (((0,), (0,)), ((), ())), preferred_element_type=jnp.float32)


def against_dot(left, weight):
    return lax.dot_general(left, weight, (((1,), (1,)), ((), ())), preferred_element_type=jnp.float32)


def assemble(zero_part, minus_one, plus_one, minus_two, plus_two, chans):
    return jnp.stack([zero_part[:, :chans], minus_one[:, :chans], zero_part[:, chans:2 * chans], plus_one[:, :chans], minus_two, minus_one[:, chans:], zero_part[:, 2 * chans:], plus_one[:, chans:], plus_two], axis=1)


def edge_terms(source_rows, target_rows, rotations, weighting, w_zero, w_one, w_two):
    chans = source_rows.shape[2]
    rotated = rotate(rotations, source_rows, False).astype(jnp.bfloat16)
    zero_in = jnp.concatenate([rotated[:, 0], rotated[:, 2], rotated[:, 6]], axis=1)
    plus_in = jnp.concatenate([rotated[:, 3], rotated[:, 7]], axis=1)
    minus_in = jnp.concatenate([rotated[:, 1], rotated[:, 5]], axis=1)
    plus_two_in = rotated[:, 8]
    minus_two_in = rotated[:, 4]
    mixed = assemble(plain_dot(zero_in, w_zero),
                     plain_dot(minus_in, w_one[0]) + plain_dot(plus_in, w_one[1]),
                     plain_dot(plus_in, w_one[0]) - plain_dot(minus_in, w_one[1]),
                     plain_dot(minus_two_in, w_two[0]) + plain_dot(plus_two_in, w_two[1]),
                     plain_dot(plus_two_in, w_two[0]) - plain_dot(minus_two_in, w_two[1]), chans)
    scaling = weighting[:, None, None]
    message = (scaling * rotate(rotations, mixed, True)).astype(jnp.bfloat16)
    upstream = (scaling * rotate(rotations, target_rows, False)).astype(jnp.bfloat16)
    zero_up = jnp.concatenate([upstream[:, 0], upstream[:, 2], upstream[:, 6]], axis=1)
    plus_up = jnp.concatenate([upstream[:, 3], upstream[:, 7]], axis=1)
    minus_up = jnp.concatenate([upstream[:, 1], upstream[:, 5]], axis=1)
    plus_two_up = upstream[:, 8]
    minus_two_up = upstream[:, 4]
    grad_zero = transposed_dot(zero_in, zero_up)
    grad_one = jnp.stack([transposed_dot(plus_in, plus_up) + transposed_dot(minus_in, minus_up),
                          transposed_dot(plus_in, minus_up) - transposed_dot(minus_in, plus_up)])
    grad_two = jnp.stack([transposed_dot(plus_two_in, plus_two_up) + transposed_dot(minus_two_in, minus_two_up),
                          transposed_dot(plus_two_in, minus_two_up) - transposed_dot(minus_two_in, plus_two_up)])
    back_mixed = assemble(against_dot(zero_up, w_zero),
                          against_dot(minus_up, w_one[0]) - against_dot(plus_up, w_one[1]),
                          against_dot(plus_up, w_one[0]) + against_dot(minus_up, w_one[1]),
                          against_dot(minus_two_up, w_two[0]) - against_dot(plus_two_up, w_two[1]),
                          against_dot(plus_two_up, w_two[0]) + against_dot(minus_two_up, w_two[1]), chans)
    backward = rotate(rotations, back_mixed, True).astype(jnp.bfloat16)
    return message, backward, grad_zero, grad_one, grad_two


def reference(coeffs, cotangent, w_zero, w_one, w_two, source, target, rotation, gate, tile_live):
    atoms_all = coeffs.shape[1]
    start_grads = (jnp.zeros(w_zero.shape, jnp.float32), jnp.zeros(w_one.shape, jnp.float32), jnp.zeros(w_two.shape, jnp.float32))

    def one_system(grads, inputs):
        coeff_sys, cot_sys, src_sys, dst_sys, rot_sys, gate_sys, live_sys = inputs
        edge_count = src_sys.shape[0]
        owner = jnp.arange(edge_count, dtype=jnp.int32) // EDGES_DEV
        global_src = (owner * A_DEV + src_sys - A_DEV).astype(jnp.int32)
        global_dst = (owner * A_DEV + dst_sys).astype(jnp.int32)
        weighting = gate_sys.astype(jnp.float32) * jnp.repeat(live_sys, TILE).astype(jnp.float32)
        rot_rows = rot_sys.astype(jnp.float32).T

        def tile_step(state, tile_index):
            rows_now = (tile_index * TILE + jnp.arange(TILE, dtype=jnp.int32)).astype(jnp.int32)

            def compute(inner):
                msg_sum, grad_sum, held = inner
                message, backward, g_zero, g_one, g_two = edge_terms(
                    coeff_sys[global_src[rows_now]], cot_sys[global_dst[rows_now]],
                    rot_rows[rows_now], weighting[rows_now], w_zero, w_one, w_two)
                msg_sum = msg_sum.at[global_dst[rows_now]].add(message.astype(jnp.float32))
                grad_sum = grad_sum.at[global_src[rows_now]].add(backward.astype(jnp.float32))
                return msg_sum, grad_sum, (held[0] + g_zero, held[1] + g_one, held[2] + g_two)

            def keep(inner):
                return inner

            return lax.cond(live_sys[tile_index] > 0, compute, keep, state), None

        begin = (jnp.zeros(coeff_sys.shape, jnp.float32), jnp.zeros(coeff_sys.shape, jnp.float32), grads)
        (msg_sum, grad_sum, grads), unused = lax.scan(tile_step, begin, jnp.arange(live_sys.shape[0], dtype=jnp.int32))
        updated = (coeff_sys.astype(jnp.float32) + msg_sum).astype(jnp.bfloat16)
        grad_coeffs = (cot_sys.astype(jnp.float32) + grad_sum).astype(jnp.bfloat16)
        return grads, (updated, grad_coeffs)

    grads, (updated, grad_coeffs) = lax.scan(one_system, start_grads, (coeffs, cotangent, source, target, rotation, gate, tile_live))
    return updated, grad_coeffs, grads[0], grads[1], grads[2]
```

```python
import jax
import jax.numpy as jnp
from jax import lax
from jax.experimental import pallas as pl
from jax.experimental.pallas import tpu as pltpu
from jax.sharding import PartitionSpec as P

MESH = pl.DeviceIdType.MESH
F32 = jnp.float32
BF16 = jnp.bfloat16

A = 64
NC = 9
C = 256
E = 1024
EB = 256
NB = E // EB
ROT = 35
TILE = 64
W9 = NC * C
ROWS = 9728
HALF = ROWS // 2
BLOCKS = ((0, 1, 0), (1, 3, 1), (10, 5, 4))
ORDER = (0, 2, 6, 3, 7, 1, 5, 8, 4)
POS = tuple(ORDER.index(c) for c in range(NC))
NATURAL = tuple(range(NC))
UNITS = (6, 6, 7)
START = (0, 1536, 3072)
AXES = (("x", "y", "z"), ("y", "z", "x"), ("z", "x", "y"))


def nn(a, b):
    return jnp.dot(a, b, preferred_element_type=F32)


def nt(a, b):
    return lax.dot_general(a, b, (((1,), (1,)), ((), ())), preferred_element_type=F32)


def eye(n):
    r = lax.broadcasted_iota(jnp.int32, (n, n), 0)
    c = lax.broadcasted_iota(jnp.int32, (n, n), 1)
    return jnp.where(r == c, 1.0, 0.0).astype(BF16)


def rotate(wide, work, in_pos, out, out_pos, lane0, inverse):
    for lt in range(EB // 128):
        lanes = pl.ds(lane0 + lt * 128, 128)
        for offset, extent, first in BLOCKS:
            d = [wide[offset + i, :, lanes][None] for i in range(extent * extent)]
            for chunk in range(0, C, 32):
                x = [
                    work[
                        pl.ds(in_pos[first + j] * C + chunk, 32), pl.ds(lt * 128, 128)
                    ].reshape(4, 8, 128)
                    for j in range(extent)
                ]
                for k in range(extent):
                    total = None
                    for j in range(extent):
                        entry = j * extent + k if inverse else k * extent + j
                        term = d[entry] * x[j]
                        total = term if total is None else total + term
                    out[pl.ds(out_pos[first + k] * C + chunk, 32), lanes] = total.reshape(
                        32, 128
                    ).astype(BF16)


def body(
    coef, cot, w0, w1, w2, src, tgt, rot, gate, live,
    upd, gco, O,
    hT, yT, X, T3, CT, cotT, W0T, M1f, M1b, M2f, M2b, wide, oh_s, oh_t,
    G, R0, S, R1, T1, R2, T2, R3, SB, RB,
    halo_s, halo_r, core_s, core_r, ring_s, ring_r,
):
    dp = lax.axis_index("dp")
    hp = lax.axis_index("help")
    x, core = dp // 2, dp % 2
    y, z = hp // 4, hp % 4
    at = {"x": x, "y": y, "z": z}

    def peer(axis, d):
        if axis == "x":
            return ((x + d) % 4 * 2 + core, hp)
        if axis == "y":
            return (dp, (y + d) % 4 * 4 + z)
        return (dp, y * 4 + (z + d) % 4)

    partner = (x * 2 + 1 - core, hp)
    above = (dp, (hp + 1) % 16)
    below = (dp, (hp + 15) % 16)

    barrier = pltpu.get_barrier_semaphore()
    peers = [partner, above, below] + [peer(a, d) for a in "xyz" for d in (1, 2, 3)]
    for device in peers:
        pl.semaphore_signal(barrier, inc=1, device_id=device, device_id_type=MESH)

    def remote(s, t, sem_s, sem_r, device):
        return pltpu.make_async_remote_copy(
            src_ref=s, dst_ref=t, send_sem=sem_s, recv_sem=sem_r,
            device_id=device, device_id_type=MESH,
        )

    halo = [
        remote(coef, T3.at[0], halo_s.at[0], halo_r.at[0], above),
        remote(coef, T3.at[1], halo_s.at[1], halo_r.at[1], below),
    ]
    give = [
        remote(SB.at[1], RB.at[0], halo_s.at[2], halo_r.at[2], above),
        remote(SB.at[0], RB.at[1], halo_s.at[3], halo_r.at[3], below),
    ]

    def half_rows(c):
        return pl.ds(pl.multiple_of(c * HALF, 256), HALF)

    swap = remote(G.at[half_rows(1 - core)], R0, core_s.at[0], core_r.at[0], partner)
    share = remote(
        O.at[half_rows(core)], O.at[half_rows(core)], core_s.at[1], core_r.at[1], partner
    )

    def ring(stage, make):
        return [
            [
                remote(*make(p, d), ring_s.at[stage, p, d - 1], ring_r.at[stage, p, d - 1], peer(AXES[p][(0, 1, 2, 1, 0)[stage]], d))
                for d in (1, 2, 3)
            ]
            for p in range(3)
        ]

    def first_make(p, d):
        q = UNITS[p] * 64
        j = (at[AXES[p][0]] + d) % 4
        return (
            S.at[pl.ds(pl.multiple_of(START[p] + j * q, 64), q)],
            R1.at[d - 1, pl.ds(START[p] // 4, q)],
        )

    def second_make(p, d):
        q = UNITS[p] * 16
        j = (at[AXES[p][1]] + d) % 4
        return (
            T1.at[pl.ds(pl.multiple_of(START[p] // 4 + j * q, 16), q)],
            R2.at[d - 1, pl.ds(START[p] // 16, q)],
        )

    def third_make(p, d):
        rows = pl.ds(START[p] // 16, UNITS[p] * 16)
        return T2.at[rows], R3.at[d - 1, rows]

    def place(p, deep):
        q = UNITS[p] * 16
        base = core * HALF + START[p] + at[AXES[p][0]] * (4 * q)
        if deep:
            return pl.ds(pl.multiple_of(base + at[AXES[p][1]] * q, 16), q)
        return pl.ds(pl.multiple_of(base, 64), 4 * q)

    def fourth_make(p, d):
        return O.at[place(p, True)], O.at[place(p, True)]

    def fifth_make(p, d):
        return O.at[place(p, False)], O.at[place(p, False)]

    stages = [
        ring(i, m)
        for i, m in enumerate((first_make, second_make, third_make, fourth_make, fifth_make))
    ]

    def start(stage):
        for part in stages[stage]:
            for copy in part:
                copy.start()

    def arrive(stage, p):
        for copy in stages[stage][p]:
            copy.wait_recv()

    wide[...] = jnp.broadcast_to(rot[...].astype(F32)[:, None, :], (ROT, 8, E))
    lane = lax.broadcasted_iota(jnp.int32, (1, E), 1) // TILE
    alive = jnp.zeros((1, E), F32)
    for t in range(E // TILE):
        alive = jnp.where(lane == t, live[0, t].astype(F32), alive)
    q = gate[...].astype(F32) * alive
    for r in range(0, 3 * A, A):
        ids = lax.broadcasted_iota(jnp.int32, (A, E), 0)
        oh_s[pl.ds(r, A), :] = jnp.where(ids + r == src[...], 1.0, 0.0).astype(BF16)
    ids = lax.broadcasted_iota(jnp.int32, (A, E), 0)
    oh_t[...] = jnp.where(ids == tgt[...], q, 0.0).astype(BF16)

    one = eye(C)
    for c in range(NC):
        cotT[pl.ds(c * C, C), :] = nt(one, cot[pl.ds(c * A, A), :]).astype(BF16)

    pl.semaphore_wait(barrier, len(peers))
    for copy in halo:
        copy.start()

    for i in range(3):
        W0T[pl.ds(i * C, C), :] = nt(one, w0[:, pl.ds(i * C, C)]).astype(BF16)
    for fwd, bwd, w, n in ((M1f, M1b, w1, 512), (M2f, M2b, w2, 256)):
        lo, hi = pl.ds(0, n), pl.ds(n, n)
        bwd[lo, lo] = w[0]
        bwd[lo, hi] = w[1]
        bwd[hi, lo] = -w[1]
        bwd[hi, hi] = w[0]
        for i in range(n // C):
            rows, next_rows = pl.ds(i * C, C), pl.ds(n + i * C, C)
            real = nt(one, w[0, :, pl.ds(i * C, C)])
            imag = nt(one, w[1, :, pl.ds(i * C, C)])
            fwd[rows, lo] = real.astype(BF16)
            fwd[rows, hi] = (-imag).astype(BF16)
            fwd[next_rows, lo] = imag.astype(BF16)
            fwd[next_rows, hi] = real.astype(BF16)

    def gather(table, onehot, out):
        def step(b, carry):
            lane0 = pl.multiple_of(b * EB, EB)
            pick = onehot[:, pl.ds(lane0, EB)]
            for c in range(NC):
                X[pl.ds(c * C, C), :] = nn(table[pl.ds(c * C, C), :], pick)
            rotate(wide, X, NATURAL, out, POS, lane0, False)
            return carry

        lax.fori_loop(0, NB, step, 0)

    gather(cotT, oh_t, hT)

    for copy in halo:
        copy.wait_recv()
    for c in range(NC):
        rows = pl.ds(c * A, A)
        both = jnp.concatenate([T3[0, rows, :], coef[rows, :], T3[1, rows, :]], axis=0)
        CT[pl.ds(c * C, C), :] = nt(one, both).astype(BF16)
    gather(CT, oh_s, yT)

    def put(base, col_rows, row0, value):
        for k in range(value.shape[1] // 128):
            G[pl.ds(base + k * col_rows + row0, value.shape[0]), :] = value[
                :, k * 128 : (k + 1) * 128
            ].astype(BF16)

    for i in range(3):
        for j in range(3):
            put(j * 2 * 768, 768, i * C, nt(yT[pl.ds(i * C, C), :], hT[pl.ds(j * C, C), :]))
    for base, a0, b0, n in ((4608, 768, 1280, 512), (8704, 1792, 2048, 256)):
        for i in range(n // C):
            ya, yb = yT[pl.ds(a0 + i * C, C), :], yT[pl.ds(b0 + i * C, C), :]
            for j in range(n // C):
                ha, hb = hT[pl.ds(a0 + j * C, C), :], hT[pl.ds(b0 + j * C, C), :]
                put(base + j * 2 * n, n, i * C, nt(ya, ha) + nt(yb, hb))
                put(base + n * n // 128 + j * 2 * n, n, i * C, nt(ya, hb) - nt(yb, ha))
    swap.start()

    def mix(zero, first, second, data, b):
        lane0 = pl.multiple_of(b * EB, EB)
        lanes = pl.ds(lane0, EB)
        for m, r0, n in ((zero, 0, 768), (first, 768, 1024), (second, 1792, 512)):
            right = data[pl.ds(r0, n), lanes]
            for i in range(n // C):
                X[pl.ds(r0 + i * C, C), :] = nn(m[pl.ds(i * C, C), :], right)
        rotate(wide, X, POS, data, NATURAL, lane0, True)

    def backward(lo, hi):
        lax.fori_loop(lo, hi, lambda b, t: (mix(w0, M1b, M2b, hT, b), t)[1], 0)

    def forward(lo, hi):
        lax.fori_loop(lo, hi, lambda b, t: (mix(W0T, M1f, M2f, yT, b), t)[1], 0)

    backward(0, 1)
    swap.wait_recv()

    def add_core(i, carry):
        rows = pl.ds(pl.multiple_of(i * 304, 16), 304)
        own = pl.ds(pl.multiple_of(core * HALF + i * 304, 16), 304)
        S[rows, :] = (G[own, :].astype(F32) + R0[rows, :].astype(F32)).astype(BF16)
        return carry

    lax.fori_loop(0, 16, add_core, 0)
    start(0)
    backward(1, 4)
    for c in range(NC):
        total = nt(oh_s[...], hT[pl.ds(c * C, C), :])
        rows = pl.ds(c * A, A)
        SB[0, rows, :] = total[0:A].astype(BF16)
        SB[1, rows, :] = total[2 * A : 3 * A].astype(BF16)
        X[rows, :] = total[A : 2 * A]
    for copy in give:
        copy.start()
    for p in range(3):
        arrive(0, p)
        n = UNITS[p] * 64
        own = pl.ds(pl.multiple_of(START[p] + at[AXES[p][0]] * n, 64), n)
        rows = pl.ds(START[p] // 4, n)
        T1[rows, :] = (S[own, :].astype(F32) + R1[1, rows, :].astype(F32)) + (
            R1[0, rows, :].astype(F32) + R1[2, rows, :].astype(F32)
        )
        for copy in stages[1][p]:
            copy.start()
    for copy in give:
        copy.wait_recv()
    gco[...] = (
        (cot[...].astype(F32) + X[pl.ds(0, NC * A), :])
        + (RB[0].astype(F32) + RB[1].astype(F32))
    ).astype(BF16)

    forward(0, 1)
    for p in range(3):
        arrive(1, p)
        n = UNITS[p] * 16
        own = pl.ds(pl.multiple_of(START[p] // 4 + at[AXES[p][1]] * n, 16), n)
        rows = pl.ds(START[p] // 16, n)
        T2[rows, :] = (T1[own, :] + R2[1, rows, :]) + (R2[0, rows, :] + R2[2, rows, :])
        for copy in stages[2][p]:
            copy.start()
    forward(1, 2)
    for p in range(3):
        arrive(2, p)
        rows = pl.ds(START[p] // 16, UNITS[p] * 16)
        O[place(p, True), :] = (
            (T2[rows, :] + R3[1, rows, :]) + (R3[0, rows, :] + R3[2, rows, :])
        ).astype(BF16)
        for copy in stages[3][p]:
            copy.start()
    forward(2, 3)
    for p in range(3):
        arrive(3, p)
        for copy in stages[4][p]:
            copy.start()
    forward(3, 4)
    for c in range(NC):
        rows = pl.ds(c * A, A)
        total = nt(oh_t[...], yT[pl.ds(c * C, C), :])
        upd[rows, :] = (coef[rows, :].astype(F32) + total).astype(BF16)
    for p in range(3):
        arrive(4, p)
    share.start()
    for copy in halo + give + [swap]:
        copy.wait_send()
    for stage in stages:
        for part in stage:
            for copy in part:
                copy.wait_send()
    share.wait()


def vmem(*shape):
    return pltpu.VMEM(shape, BF16)


def work(coef, cot, w0, w1, w2, src, tgt, rot, gate, live):
    whole = pl.BlockSpec(memory_space=pltpu.VMEM)
    return pl.pallas_call(
        body,
        out_shape=(
            jax.ShapeDtypeStruct((NC * A, C), BF16),
            jax.ShapeDtypeStruct((NC * A, C), BF16),
            jax.ShapeDtypeStruct((ROWS, 128), BF16),
        ),
        in_specs=[whole] * 9 + [pl.BlockSpec(memory_space=pltpu.SMEM)],
        out_specs=(whole,) * 3,
        scratch_shapes=[
            vmem(W9, E),
            vmem(W9, E),
            pltpu.VMEM((W9, EB), F32),
            vmem(2, NC * A, C),
            vmem(W9, 3 * A),
            vmem(W9, A),
            vmem(768, 768),
            vmem(1024, 1024),
            vmem(1024, 1024),
            vmem(512, 512),
            vmem(512, 512),
            pltpu.VMEM((ROT, 8, E), F32),
            vmem(3 * A, E),
            vmem(A, E),
            vmem(ROWS, 128),
            vmem(HALF, 128),
            vmem(HALF, 128),
            vmem(3, HALF // 4, 128),
            pltpu.VMEM((HALF // 4, 128), F32),
            pltpu.VMEM((3, HALF // 16, 128), F32),
            pltpu.VMEM((HALF // 16, 128), F32),
            pltpu.VMEM((3, HALF // 16, 128), F32),
            vmem(2, NC * A, C),
            vmem(2, NC * A, C),
            pltpu.SemaphoreType.DMA((4,)),
            pltpu.SemaphoreType.DMA((4,)),
            pltpu.SemaphoreType.DMA((2,)),
            pltpu.SemaphoreType.DMA((2,)),
            pltpu.SemaphoreType.DMA((5, 3, 3)),
            pltpu.SemaphoreType.DMA((5, 3, 3)),
        ],
        compiler_params=pltpu.CompilerParams(
            collective_id=0, has_side_effects=True, vmem_limit_bytes=56 * 2**20
        ),
        name="layer",
    )(coef, cot, w0, w1, w2, src, tgt, rot, gate, live)


def shards(coeffs, cotangent, w_zero, w_one, w_two, source, target, rotation, gate, tile_live):
    def by_coef(rows):
        return jnp.transpose(rows[0], (1, 0, 2)).reshape(NC * A, C)

    def by_atom(rows):
        return jnp.transpose(rows.reshape(NC, A, C), (1, 0, 2))[None]

    upd, gco, grads = work(
        by_coef(coeffs), by_coef(cotangent), w_zero, w_one, w_two,
        source, target, rotation[0], gate, tile_live,
    )
    zero = grads[:4608].reshape(6, 768, 128).transpose(1, 0, 2).reshape(768, 768)
    one = grads[4608:8704].reshape(2, 4, 512, 128).transpose(0, 2, 1, 3).reshape(2, 512, 512)
    two = grads[8704:].reshape(2, 2, 256, 128).transpose(0, 2, 1, 3).reshape(2, 256, 256)
    return by_atom(upd), by_atom(gco), zero.astype(F32), one.astype(F32), two.astype(F32)


def solution(mesh):
    return jax.shard_map(
        shards,
        mesh=mesh,
        in_specs=(
            P("dp", "help", None, None),
            P("dp", "help", None, None),
            P(),
            P(),
            P(),
            P("dp", "help"),
            P("dp", "help"),
            P("dp", None, "help"),
            P("dp", "help"),
            P("dp", "help"),
        ),
        out_specs=(P("dp", "help", None, None), P("dp", "help", None, None), P(), P(), P()),
        check_vma=False,
    )
```

```python
import jax
import jax.numpy as jnp
from jax import lax
from jax.experimental import pallas as pl
from jax.experimental.pallas import tpu as pltpu
from jax.sharding import PartitionSpec as P

MESH = pl.DeviceIdType.MESH
F32 = jnp.float32
BF16 = jnp.bfloat16

A = 64
NC = 9
C = 256
E = 1024
EB = 256
NB = E // EB
ROT = 35
TILE = 64
W9 = NC * C
ROWS = 9728
HALF = ROWS // 2
BLOCKS = ((0, 1, 0), (1, 3, 1), (10, 5, 4))
ORDER = (0, 2, 6, 3, 7, 1, 5, 8, 4)
POS = tuple(ORDER.index(c) for c in range(NC))
NATURAL = tuple(range(NC))
UNITS = (6, 7, 6)
START = (0, 1536, 3328)
AXES = (("x", "y", "z"), ("y", "z", "x"), ("z", "x", "y"))


def nn(a, b):
    return jnp.dot(a, b, preferred_element_type=F32)


def nt(a, b):
    return lax.dot_general(a, b, (((1,), (1,)), ((), ())), preferred_element_type=F32)


def eye(n):
    r = lax.broadcasted_iota(jnp.int32, (n, n), 0)
    c = lax.broadcasted_iota(jnp.int32, (n, n), 1)
    return jnp.where(r == c, 1.0, 0.0).astype(BF16)


def rotate(wide, work, in_pos, out, out_pos, lane0, inverse, degrees=(0, 1, 2)):
    for lt in range(EB // 128):
        lanes = pl.ds(lane0 + lt * 128, 128)
        for offset, extent, first in [BLOCKS[g] for g in degrees]:
            d = [wide[offset + i, :, lanes][None] for i in range(extent * extent)]
            for chunk in range(0, C, 32):
                x = [
                    work[
                        pl.ds(in_pos[first + j] * C + chunk, 32), pl.ds(lt * 128, 128)
                    ].reshape(4, 8, 128)
                    for j in range(extent)
                ]
                for k in range(extent):
                    total = None
                    for j in range(extent):
                        entry = j * extent + k if inverse else k * extent + j
                        term = d[entry] * x[j]
                        total = term if total is None else total + term
                    out[pl.ds(out_pos[first + k] * C + chunk, 32), lanes] = total.reshape(
                        32, 128
                    ).astype(BF16)


def body(
    coef, cot, w0_in, w1_in, w2_in, src, tgt, rot, gate, live,
    upd, gco, O,
    w0, w1, w2, hT, yT, bT, X, own_sum, T3, CT, cotT, W0T, M1f, M1b, M2f, M2b, wide, oh_s, oh_t,
    G, R0, S, R1, T1, R2, T2, R3, SB, RB,
    halo_s, halo_r, core_s, core_r, ring_s, ring_r, load_sem,
):
    dp = lax.axis_index("dp")
    hp = lax.axis_index("help")
    x, core = dp // 2, dp % 2
    y, z = hp // 4, hp % 4
    at = {"x": x, "y": y, "z": z}

    def peer(axis, d):
        if axis == "x":
            return ((x + d) % 4 * 2 + core, hp)
        if axis == "y":
            return (dp, (y + d) % 4 * 4 + z)
        return (dp, y * 4 + (z + d) % 4)

    partner = (x * 2 + 1 - core, hp)
    above = (dp, (hp + 1) % 16)
    below = (dp, (hp + 15) % 16)

    barrier = pltpu.get_barrier_semaphore()
    peers = [partner, above, below] + [peer(a, d) for a in "xyz" for d in (1, 2, 3)]
    for device in peers:
        pl.semaphore_signal(barrier, inc=1, device_id=device, device_id_type=MESH)

    def remote(s, t, sem_s, sem_r, device):
        return pltpu.make_async_remote_copy(
            src_ref=s, dst_ref=t, send_sem=sem_s, recv_sem=sem_r,
            device_id=device, device_id_type=MESH,
        )

    halo = [
        [
            remote(coef.at[rows], T3.at[0, rows], halo_s.at[0, i], halo_r.at[0, i], above),
            remote(coef.at[rows], T3.at[1, rows], halo_s.at[1, i], halo_r.at[1, i], below),
        ]
        for i, rows in enumerate((pl.ds(0, 4 * A), pl.ds(4 * A, 5 * A)))
    ]
    give = [
        remote(SB.at[1], RB.at[0], halo_s.at[2, 0], halo_r.at[2, 0], above),
        remote(SB.at[0], RB.at[1], halo_s.at[2, 1], halo_r.at[2, 1], below),
    ]
    loads = [
        pltpu.make_async_copy(far, near, load_sem.at[i])
        for i, (far, near) in enumerate(((w0_in, w0), (w1_in, w1), (w2_in, w2)))
    ]
    for copy in loads:
        copy.start()

    swap = [
        remote(
            G.at[pl.ds(pl.multiple_of((1 - core) * HALF + START[p], 256), UNITS[p] * 256)],
            R0.at[pl.ds(START[p], UNITS[p] * 256)],
            core_s.at[4, p], core_r.at[4, p], partner,
        )
        for p in range(3)
    ]

    def quarter(p, d):
        n = UNITS[p] * 64
        row = core * HALF + START[p] + (at[AXES[p][0]] + 4 - d) % 4 * n
        return O.at[pl.ds(pl.multiple_of(row, 64), n)]

    share = [
        [
            remote(quarter(p, d), quarter(p, d), core_s.at[d, p], core_r.at[d, p], partner)
            for d in range(4)
        ]
        for p in range(3)
    ]

    def ring(stage, make):
        return [
            [
                remote(*make(p, d), ring_s.at[stage, p, d - 1], ring_r.at[stage, p, d - 1], peer(AXES[p][(0, 1, 2, 1, 0)[stage]], d))
                for d in (1, 2, 3)
            ]
            for p in range(3)
        ]

    def first_make(p, d):
        q = UNITS[p] * 64
        j = (at[AXES[p][0]] + d) % 4
        return (
            S.at[pl.ds(pl.multiple_of(START[p] + j * q, 64), q)],
            R1.at[d - 1, pl.ds(START[p] // 4, q)],
        )

    def second_make(p, d):
        q = UNITS[p] * 16
        j = (at[AXES[p][1]] + d) % 4
        return (
            T1.at[pl.ds(pl.multiple_of(START[p] // 4 + j * q, 16), q)],
            R2.at[d - 1, pl.ds(START[p] // 16, q)],
        )

    def third_make(p, d):
        rows = pl.ds(START[p] // 16, UNITS[p] * 16)
        return T2.at[rows], R3.at[d - 1, rows]

    def place(p, deep):
        q = UNITS[p] * 16
        base = core * HALF + START[p] + at[AXES[p][0]] * (4 * q)
        if deep:
            return pl.ds(pl.multiple_of(base + at[AXES[p][1]] * q, 16), q)
        return pl.ds(pl.multiple_of(base, 64), 4 * q)

    def fourth_make(p, d):
        return O.at[place(p, True)], O.at[place(p, True)]

    def fifth_make(p, d):
        return O.at[place(p, False)], O.at[place(p, False)]

    stages = [
        ring(i, m)
        for i, m in enumerate((first_make, second_make, third_make, fourth_make, fifth_make))
    ]

    def go(stage, p):
        for copy in stages[stage][p]:
            copy.start()

    def arrive(stage, p):
        for copy in stages[stage][p]:
            copy.wait_recv()

    def advance(k, p):
        n = UNITS[p] * 64
        if k == 0:
            swap[p].wait_recv()

            def add_core(i, carry):
                rows = pl.ds(pl.multiple_of(START[p] + i * n, 64), n)
                own = pl.ds(pl.multiple_of(core * HALF + START[p] + i * n, 64), n)
                S[rows, :] = (G[own, :].astype(F32) + R0[rows, :].astype(F32)).astype(BF16)
                return carry

            lax.fori_loop(0, 4, add_core, 0)
            go(0, p)
        elif k == 1:
            arrive(0, p)
            own = pl.ds(pl.multiple_of(START[p] + at[AXES[p][0]] * n, 64), n)
            rows = pl.ds(START[p] // 4, n)
            T1[rows, :] = (S[own, :].astype(F32) + R1[1, rows, :].astype(F32)) + (
                R1[0, rows, :].astype(F32) + R1[2, rows, :].astype(F32)
            )
            go(1, p)
        elif k == 2:
            arrive(1, p)
            n = n // 4
            own = pl.ds(pl.multiple_of(START[p] // 4 + at[AXES[p][1]] * n, 16), n)
            rows = pl.ds(START[p] // 16, n)
            T2[rows, :] = (T1[own, :] + R2[1, rows, :]) + (R2[0, rows, :] + R2[2, rows, :])
            go(2, p)
        elif k == 3:
            arrive(2, p)
            rows = pl.ds(START[p] // 16, n // 4)
            O[place(p, True), :] = (
                (T2[rows, :] + R3[1, rows, :]) + (R3[0, rows, :] + R3[2, rows, :])
            ).astype(BF16)
            go(3, p)
        elif k == 4:
            arrive(3, p)
            go(4, p)
            share[p][0].start()
        else:
            for d in (1, 2, 3):
                stages[4][p][d - 1].wait_recv()
                share[p][d].start()

    wide[...] = jnp.broadcast_to(rot[...].astype(F32)[:, None, :], (ROT, 8, E))
    lane = lax.broadcasted_iota(jnp.int32, (1, E), 1) // TILE
    alive = jnp.zeros((1, E), F32)
    for t in range(E // TILE):
        alive = jnp.where(lane == t, live[0, t].astype(F32), alive)
    q = gate[...].astype(F32) * alive
    for r in range(0, 3 * A, A):
        ids = lax.broadcasted_iota(jnp.int32, (A, E), 0)
        oh_s[pl.ds(r, A), :] = jnp.where(ids + r == src[...], 1.0, 0.0).astype(BF16)
    ids = lax.broadcasted_iota(jnp.int32, (A, E), 0)
    oh_t[...] = jnp.where(ids == tgt[...], q, 0.0).astype(BF16)

    pl.semaphore_wait(barrier, len(peers))
    for pair in halo:
        for copy in pair:
            copy.start()

    one = eye(C)
    for c in range(NC):
        cotT[pl.ds(c * C, C), :] = nt(one, cot[pl.ds(c * A, A), :]).astype(BF16)
    for copy in loads:
        copy.wait()
    for i in range(3):
        W0T[pl.ds(i * C, C), :] = nt(one, w0[:, pl.ds(i * C, C)]).astype(BF16)
    for fwd, bwd, w, n in ((M1f, M1b, w1, 512), (M2f, M2b, w2, 256)):
        lo, hi = pl.ds(0, n), pl.ds(n, n)
        bwd[lo, lo] = w[0]
        bwd[lo, hi] = w[1]
        bwd[hi, lo] = -w[1]
        bwd[hi, hi] = w[0]
        for i in range(n // C):
            rows, next_rows = pl.ds(i * C, C), pl.ds(n + i * C, C)
            real = nt(one, w[0, :, pl.ds(i * C, C)])
            imag = nt(one, w[1, :, pl.ds(i * C, C)])
            fwd[rows, lo] = real.astype(BF16)
            fwd[rows, hi] = (-imag).astype(BF16)
            fwd[next_rows, lo] = imag.astype(BF16)
            fwd[next_rows, hi] = real.astype(BF16)

    def gather(table, onehot, out, degrees):
        def step(b, carry):
            lane0 = pl.multiple_of(b * EB, EB)
            pick = onehot[:, pl.ds(lane0, EB)]
            for g in degrees:
                for c in range(g * g, (g + 1) * (g + 1)):
                    X[pl.ds(c * C, C), :] = nn(table[pl.ds(c * C, C), :], pick)
                rotate(wide, X, NATURAL, out, POS, lane0, False, (g,))
            return carry

        lax.fori_loop(0, NB, step, 0)

    def mix(zero, first, second, data, out, b):
        lane0 = pl.multiple_of(b * EB, EB)
        lanes = pl.ds(lane0, EB)
        for m, r0, n in ((zero, 0, 768), (first, 768, 1024), (second, 1792, 512)):
            right = data[pl.ds(r0, n), lanes]
            for i in range(n // C):
                X[pl.ds(r0 + i * C, C), :] = nn(m[pl.ds(i * C, C), :], right)
        rotate(wide, X, POS, out, NATURAL, lane0, True)

    def backward(lo, hi):
        lax.fori_loop(lo, hi, lambda b, t: (mix(w0, M1b, M2b, hT, bT, b), t)[1], 0)

    def forward(lo, hi):
        lax.fori_loop(lo, hi, lambda b, t: (mix(W0T, M1f, M2f, yT, yT, b), t)[1], 0)

    gather(cotT, oh_t, hT, (0, 1, 2))
    backward(0, 1)

    def table(i, coefs):
        for copy in halo[i]:
            copy.wait_recv()
        for c in coefs:
            rows = pl.ds(c * A, A)
            both = jnp.concatenate([T3[0, rows, :], coef[rows, :], T3[1, rows, :]], axis=0)
            CT[pl.ds(c * C, C), :] = nt(one, both).astype(BF16)

    def put(tile, value):
        for k in range(2):
            G[pl.ds(k * HALF + tile * C, C), :] = value[:, k * 128 : (k + 1) * 128].astype(BF16)

    def zero_tiles(tile, i):
        for j in range(3):
            put(tile + j, nt(yT[pl.ds(i * C, C), :], hT[pl.ds(j * C, C), :]))

    def pair_tiles(tile, a0, b0, n, i):
        ya, yb = yT[pl.ds(a0 + i * C, C), :], yT[pl.ds(b0 + i * C, C), :]
        for j in range(n):
            ha, hb = hT[pl.ds(a0 + j * C, C), :], hT[pl.ds(b0 + j * C, C), :]
            put(tile + j, nt(ya, ha) + nt(yb, hb))
            put(tile + n + j, nt(ya, hb) - nt(yb, ha))

    table(0, range(4))
    gather(CT, oh_s, yT, (0, 1))
    zero_tiles(0, 0)
    zero_tiles(3, 1)
    swap[0].start()
    pair_tiles(6, 768, 1280, 2, 0)
    table(1, range(4, 9))
    gather(CT, oh_s, yT, (2,))
    advance(0, 0)
    zero_tiles(10, 2)
    swap[1].start()
    pair_tiles(13, 768, 1280, 2, 1)
    pair_tiles(17, 1792, 2048, 1, 0)
    swap[2].start()
    advance(0, 1)
    backward(1, 2)
    advance(0, 2)
    advance(1, 0)
    backward(2, 4)
    advance(1, 1)

    def sum_back(coefs):
        for c in coefs:
            total = nt(oh_s[...], bT[pl.ds(c * C, C), :])
            rows = pl.ds(c * A, A)
            SB[0, rows, :] = total[0:A].astype(BF16)
            SB[1, rows, :] = total[2 * A : 3 * A].astype(BF16)
            own_sum[rows, :] = total[A : 2 * A]

    sum_back(range(5))
    advance(2, 0)
    advance(1, 2)
    sum_back(range(5, 9))
    for copy in give:
        copy.start()
    forward(0, 1)
    advance(2, 1)
    advance(3, 0)
    forward(1, 2)
    advance(2, 2)
    forward(2, 3)
    advance(3, 1)
    advance(4, 0)
    forward(3, 4)
    advance(3, 2)
    advance(4, 1)
    for c in range(NC):
        rows = pl.ds(c * A, A)
        total = nt(oh_t[...], yT[pl.ds(c * C, C), :])
        upd[rows, :] = (coef[rows, :].astype(F32) + total).astype(BF16)
    for copy in give:
        copy.wait_recv()
    gco[...] = (
        (cot[...].astype(F32) + own_sum[...]) + (RB[0].astype(F32) + RB[1].astype(F32))
    ).astype(BF16)
    advance(5, 0)
    advance(4, 2)
    advance(5, 1)
    advance(5, 2)
    for copy in halo[0] + halo[1] + give + swap:
        copy.wait_send()
    for stage in stages:
        for part in stage:
            for copy in part:
                copy.wait_send()
    for part in share:
        for copy in part:
            copy.wait()


def finish(upd, gco, O, upd_out, gco_out, g_zero, g_one, g_two):
    upd_out[...] = upd[...]
    gco_out[...] = gco[...]

    def tile(t, out, row, col):
        for k in range(2):
            out[pl.ds(row * C, C), pl.ds(col * C + k * 128, 128)] = O[
                pl.ds(k * HALF + t * C, C), :
            ].astype(F32)

    for j in range(3):
        for i, t in enumerate((0, 3, 10)):
            tile(t + j, g_zero, i, j)
    for part in range(2):
        for j in range(2):
            for i, t in enumerate((6, 13)):
                tile(t + 2 * part + j, g_one.at[part], i, j)
        tile(17 + part, g_two.at[part], 0, 0)


def vmem(*shape):
    return pltpu.VMEM(shape, BF16)


def work(coef, cot, w0, w1, w2, src, tgt, rot, gate, live):
    whole = pl.BlockSpec(memory_space=pltpu.VMEM)
    return pl.pallas_call(
        body,
        out_shape=(
            jax.ShapeDtypeStruct((NC * A, C), BF16),
            jax.ShapeDtypeStruct((NC * A, C), BF16),
            jax.ShapeDtypeStruct((ROWS, 128), BF16),
        ),
        in_specs=[whole] * 2
        + [pl.BlockSpec(memory_space=pl.ANY)] * 3
        + [whole] * 4
        + [pl.BlockSpec(memory_space=pltpu.SMEM)],
        out_specs=(whole,) * 3,
        scratch_shapes=[
            vmem(768, 768),
            vmem(2, 512, 512),
            vmem(2, 256, 256),
            vmem(W9, E),
            vmem(W9, E),
            vmem(W9, E),
            pltpu.VMEM((W9, EB), F32),
            pltpu.VMEM((NC * A, C), F32),
            vmem(2, NC * A, C),
            vmem(W9, 3 * A),
            vmem(W9, A),
            vmem(768, 768),
            vmem(1024, 1024),
            vmem(1024, 1024),
            vmem(512, 512),
            vmem(512, 512),
            pltpu.VMEM((ROT, 8, E), F32),
            vmem(3 * A, E),
            vmem(A, E),
            vmem(ROWS, 128),
            vmem(HALF, 128),
            vmem(HALF, 128),
            vmem(3, HALF // 4, 128),
            pltpu.VMEM((HALF // 4, 128), F32),
            pltpu.VMEM((3, HALF // 16, 128), F32),
            pltpu.VMEM((HALF // 16, 128), F32),
            pltpu.VMEM((3, HALF // 16, 128), F32),
            vmem(2, NC * A, C),
            vmem(2, NC * A, C),
            pltpu.SemaphoreType.DMA((3, 2)),
            pltpu.SemaphoreType.DMA((3, 2)),
            pltpu.SemaphoreType.DMA((5, 3)),
            pltpu.SemaphoreType.DMA((5, 3)),
            pltpu.SemaphoreType.DMA((5, 3, 3)),
            pltpu.SemaphoreType.DMA((5, 3, 3)),
            pltpu.SemaphoreType.DMA((3,)),
        ],
        compiler_params=pltpu.CompilerParams(
            collective_id=0, has_side_effects=True, vmem_limit_bytes=56 * 2**20
        ),
        name="layer",
    )(coef, cot, w0, w1, w2, src, tgt, rot, gate, live)


def shards(coeffs, cotangent, w_zero, w_one, w_two, source, target, rotation, gate, tile_live):
    def by_coef(rows):
        return jnp.transpose(rows[0], (1, 0, 2)).reshape(NC * A, C)

    def by_atom(rows):
        return jnp.transpose(rows.reshape(NC, A, C), (1, 0, 2))[None]

    upd, gco, grads = work(
        by_coef(coeffs), by_coef(cotangent), w_zero, w_one, w_two,
        source, target, rotation[0], gate, tile_live,
    )
    whole = pl.BlockSpec(memory_space=pltpu.VMEM)
    upd, gco, zero, one, two = pl.pallas_call(
        finish,
        out_shape=(
            jax.ShapeDtypeStruct((NC * A, C), BF16),
            jax.ShapeDtypeStruct((NC * A, C), BF16),
            jax.ShapeDtypeStruct((768, 768), F32),
            jax.ShapeDtypeStruct((2, 512, 512), F32),
            jax.ShapeDtypeStruct((2, 256, 256), F32),
        ),
        in_specs=[whole] * 3,
        out_specs=(whole,) * 5,
        compiler_params=pltpu.CompilerParams(vmem_limit_bytes=24 * 2**20),
        name="finish",
    )(upd, gco, grads)
    return by_atom(upd), by_atom(gco), zero, one, two


def solution(mesh):
    return jax.shard_map(
        shards,
        mesh=mesh,
        in_specs=(
            P("dp", "help", None, None),
            P("dp", "help", None, None),
            P(),
            P(),
            P(),
            P("dp", "help"),
            P("dp", "help"),
            P("dp", None, "help"),
            P("dp", "help"),
            P("dp", "help"),
        ),
        out_specs=(P("dp", "help", None, None), P("dp", "help", None, None), P(), P(), P()),
        check_vma=False,
    )
```

```python
import jax
import jax.numpy as jnp
from jax import lax
from jax.experimental import pallas as pl
from jax.experimental.pallas import tpu as pltpu
from jax.sharding import PartitionSpec as P

MESH = pl.DeviceIdType.MESH
F32 = jnp.float32
BF16 = jnp.bfloat16

A = 64
NC = 9
C = 256
E = 1024
EB = 256
NB = E // EB
ROT = 35
TILE = 64
W9 = NC * C
ROWS = 9728
HALF = ROWS // 2
BLOCKS = ((0, 1, 0), (1, 3, 1), (10, 5, 4))
ORDER = (0, 2, 6, 3, 7, 1, 5, 8, 4)
POS = tuple(ORDER.index(c) for c in range(NC))
NATURAL = tuple(range(NC))
UNITS = (6, 7, 6)
START = (0, 1536, 3328)
AXES = (("x", "y", "z"), ("y", "z", "x"), ("z", "x", "y"))


def nn(a, b):
    return jnp.dot(a, b, preferred_element_type=F32)


def nt(a, b):
    return lax.dot_general(a, b, (((1,), (1,)), ((), ())), preferred_element_type=F32)


def eye(n):
    r = lax.broadcasted_iota(jnp.int32, (n, n), 0)
    c = lax.broadcasted_iota(jnp.int32, (n, n), 1)
    return jnp.where(r == c, 1.0, 0.0).astype(BF16)


def rotate(wide, work, in_pos, out, out_pos, lane0, inverse, degrees=(0, 1, 2)):
    for lt in range(EB // 128):
        lanes = pl.ds(lane0 + lt * 128, 128)
        for offset, extent, first in [BLOCKS[g] for g in degrees]:
            d = [wide[offset + i, :, lanes][None] for i in range(extent * extent)]
            for chunk in range(0, C, 32):
                x = [
                    work[
                        pl.ds(in_pos[first + j] * C + chunk, 32), pl.ds(lt * 128, 128)
                    ].reshape(4, 8, 128)
                    for j in range(extent)
                ]
                for k in range(extent):
                    total = None
                    for j in range(extent):
                        entry = j * extent + k if inverse else k * extent + j
                        term = d[entry] * x[j]
                        total = term if total is None else total + term
                    out[pl.ds(out_pos[first + k] * C + chunk, 32), lanes] = total.reshape(
                        32, 128
                    ).astype(BF16)


def body(
    coef_in, cot_in, w0_in, w1_in, w2_in, rot_in, src, tgt, gate, live,
    upd_out, gco_out, O_out,
    coef, cot, rot, upd, gco, O, w0, w1, w2, hT, yT, bT, X, own_sum, T3, CT, cotT, W0T, M1f, M1b, M2f, M2b, wide, oh_s, oh_t,
    G, R0, S, R1, T1, R2, T2, R3, SB, RB,
    halo_s, halo_r, core_s, core_r, ring_s, ring_r, load_sem, store_sem,
):
    dp = lax.axis_index("dp")
    hp = lax.axis_index("help")
    x, core = dp // 2, dp % 2
    y, z = hp // 4, hp % 4
    at = {"x": x, "y": y, "z": z}

    def peer(axis, d):
        if axis == "x":
            return ((x + d) % 4 * 2 + core, hp)
        if axis == "y":
            return (dp, (y + d) % 4 * 4 + z)
        return (dp, y * 4 + (z + d) % 4)

    partner = (x * 2 + 1 - core, hp)
    above = (dp, (hp + 1) % 16)
    below = (dp, (hp + 15) % 16)

    barrier = pltpu.get_barrier_semaphore()
    peers = [partner, above, below] + [peer(a, d) for a in "xyz" for d in (1, 2, 3)]
    for device in peers:
        pl.semaphore_signal(barrier, inc=1, device_id=device, device_id_type=MESH)

    def remote(s, t, sem_s, sem_r, device):
        return pltpu.make_async_remote_copy(
            src_ref=s, dst_ref=t, send_sem=sem_s, recv_sem=sem_r,
            device_id=device, device_id_type=MESH,
        )

    halo = [
        [
            remote(coef_in.at[rows], T3.at[0, rows], halo_s.at[0, i], halo_r.at[0, i], above),
            remote(coef_in.at[rows], T3.at[1, rows], halo_s.at[1, i], halo_r.at[1, i], below),
        ]
        for i, rows in enumerate((pl.ds(0, 4 * A), pl.ds(4 * A, 5 * A)))
    ]
    give = [
        [
            remote(SB.at[1, rows], RB.at[0, rows], halo_s.at[0, i], halo_r.at[0, i], above),
            remote(SB.at[0, rows], RB.at[1, rows], halo_s.at[1, i], halo_r.at[1, i], below),
        ]
        for i, rows in ((2 + i, pl.ds(3 * A * i, 3 * A)) for i in range(3))
    ]
    loads = [
        pltpu.make_async_copy(far, near, load_sem.at[i])
        for i, (far, near) in enumerate(
            ((cot_in, cot), (rot_in, rot), (coef_in, coef), (w0_in, w0), (w1_in, w1), (w2_in, w2))
        )
    ]
    for copy in loads:
        copy.start()

    def stored(half, p):
        rows = pl.ds(pl.multiple_of(half * HALF + START[p], 256), UNITS[p] * 256)
        return O.at[rows], O_out.at[rows]

    stores = [
        pltpu.make_async_copy(*pair, store_sem.at[i])
        for i, pair in enumerate(
            [stored(core, p) for p in range(3)]
            + [stored(1 - core, p) for p in range(3)]
            + [(upd, upd_out), (gco, gco_out)]
        )
    ]

    swap = [
        remote(
            G.at[pl.ds(pl.multiple_of((1 - core) * HALF + START[p], 256), UNITS[p] * 256)],
            R0.at[pl.ds(START[p], UNITS[p] * 256)],
            core_s.at[4, p], core_r.at[4, p], partner,
        )
        for p in range(3)
    ]

    def quarter(p, d):
        n = UNITS[p] * 64
        row = core * HALF + START[p] + (at[AXES[p][0]] + 4 - d) % 4 * n
        return O.at[pl.ds(pl.multiple_of(row, 64), n)]

    share = [
        [
            remote(quarter(p, d), quarter(p, d), core_s.at[d, p], core_r.at[d, p], partner)
            for d in range(4)
        ]
        for p in range(3)
    ]

    def ring(stage, make):
        return [
            [
                remote(*make(p, d), ring_s.at[stage, p, d - 1], ring_r.at[stage, p, d - 1], peer(AXES[p][(0, 1, 2, 1, 0)[stage]], d))
                for d in (1, 2, 3)
            ]
            for p in range(3)
        ]

    def first_make(p, d):
        q = UNITS[p] * 64
        j = (at[AXES[p][0]] + d) % 4
        return (
            S.at[pl.ds(pl.multiple_of(START[p] + j * q, 64), q)],
            R1.at[d - 1, pl.ds(START[p] // 4, q)],
        )

    def second_make(p, d):
        q = UNITS[p] * 16
        j = (at[AXES[p][1]] + d) % 4
        return (
            T1.at[pl.ds(pl.multiple_of(START[p] // 4 + j * q, 16), q)],
            R2.at[d - 1, pl.ds(START[p] // 16, q)],
        )

    def third_make(p, d):
        rows = pl.ds(START[p] // 16, UNITS[p] * 16)
        return T2.at[rows], R3.at[d - 1, rows]

    def place(p, deep):
        q = UNITS[p] * 16
        base = core * HALF + START[p] + at[AXES[p][0]] * (4 * q)
        if deep:
            return pl.ds(pl.multiple_of(base + at[AXES[p][1]] * q, 16), q)
        return pl.ds(pl.multiple_of(base, 64), 4 * q)

    def fourth_make(p, d):
        return O.at[place(p, True)], O.at[place(p, True)]

    def fifth_make(p, d):
        return O.at[place(p, False)], O.at[place(p, False)]

    stages = [
        ring(i, m)
        for i, m in enumerate((first_make, second_make, third_make, fourth_make, fifth_make))
    ]

    def go(stage, p):
        for copy in stages[stage][p]:
            copy.start()

    def arrive(stage, p):
        for copy in stages[stage][p]:
            copy.wait_recv()

    def advance(k, p):
        n = UNITS[p] * 64
        if k == 0:
            swap[p].wait_recv()

            def add_core(i, carry):
                rows = pl.ds(pl.multiple_of(START[p] + i * n, 64), n)
                own = pl.ds(pl.multiple_of(core * HALF + START[p] + i * n, 64), n)
                S[rows, :] = (G[own, :].astype(F32) + R0[rows, :].astype(F32)).astype(BF16)
                return carry

            lax.fori_loop(0, 4, add_core, 0)
            go(0, p)
        elif k == 1:
            arrive(0, p)
            own = pl.ds(pl.multiple_of(START[p] + at[AXES[p][0]] * n, 64), n)
            rows = pl.ds(START[p] // 4, n)
            T1[rows, :] = (S[own, :].astype(F32) + R1[1, rows, :].astype(F32)) + (
                R1[0, rows, :].astype(F32) + R1[2, rows, :].astype(F32)
            )
            go(1, p)
        elif k == 2:
            arrive(1, p)
            n = n // 4
            own = pl.ds(pl.multiple_of(START[p] // 4 + at[AXES[p][1]] * n, 16), n)
            rows = pl.ds(START[p] // 16, n)
            T2[rows, :] = (T1[own, :] + R2[1, rows, :]) + (R2[0, rows, :] + R2[2, rows, :])
            go(2, p)
        elif k == 3:
            arrive(2, p)
            rows = pl.ds(START[p] // 16, n // 4)
            O[place(p, True), :] = (
                (T2[rows, :] + R3[1, rows, :]) + (R3[0, rows, :] + R3[2, rows, :])
            ).astype(BF16)
            go(3, p)
        elif k == 4:
            arrive(3, p)
            go(4, p)
            share[p][0].start()
        else:
            for d in (1, 2, 3):
                stages[4][p][d - 1].wait_recv()
                share[p][d].start()
            stores[p].start()

    pl.semaphore_wait(barrier, len(peers))
    for pair in halo:
        for copy in pair:
            copy.start()

    loads[0].wait()
    loads[1].wait()
    wide[...] = jnp.broadcast_to(rot[...].astype(F32)[:, None, :], (ROT, 8, E))
    lane = lax.broadcasted_iota(jnp.int32, (1, E), 1) // TILE
    alive = jnp.zeros((1, E), F32)
    for t in range(E // TILE):
        alive = jnp.where(lane == t, live[0, t].astype(F32), alive)
    q = gate[...].astype(F32) * alive
    for r in range(0, 3 * A, A):
        ids = lax.broadcasted_iota(jnp.int32, (A, E), 0)
        oh_s[pl.ds(r, A), :] = jnp.where(ids + r == src[...], 1.0, 0.0).astype(BF16)
    ids = lax.broadcasted_iota(jnp.int32, (A, E), 0)
    oh_t[...] = jnp.where(ids == tgt[...], q, 0.0).astype(BF16)

    one = eye(C)
    for c in range(NC):
        cotT[pl.ds(c * C, C), :] = nt(one, cot[pl.ds(c * A, A), :]).astype(BF16)
    for copy in loads[2:]:
        copy.wait()
    for i in range(3):
        W0T[pl.ds(i * C, C), :] = nt(one, w0[:, pl.ds(i * C, C)]).astype(BF16)
    for fwd, bwd, w, n in ((M1f, M1b, w1, 512), (M2f, M2b, w2, 256)):
        lo, hi = pl.ds(0, n), pl.ds(n, n)
        bwd[lo, lo] = w[0]
        bwd[lo, hi] = w[1]
        bwd[hi, lo] = -w[1]
        bwd[hi, hi] = w[0]
        for i in range(n // C):
            rows, next_rows = pl.ds(i * C, C), pl.ds(n + i * C, C)
            real = nt(one, w[0, :, pl.ds(i * C, C)])
            imag = nt(one, w[1, :, pl.ds(i * C, C)])
            fwd[rows, lo] = real.astype(BF16)
            fwd[rows, hi] = (-imag).astype(BF16)
            fwd[next_rows, lo] = imag.astype(BF16)
            fwd[next_rows, hi] = real.astype(BF16)

    def gather(table, onehot, out, degrees):
        def step(b, carry):
            lane0 = pl.multiple_of(b * EB, EB)
            pick = onehot[:, pl.ds(lane0, EB)]
            for g in degrees:
                for c in range(g * g, (g + 1) * (g + 1)):
                    X[pl.ds(c * C, C), :] = nn(table[pl.ds(c * C, C), :], pick)
                rotate(wide, X, NATURAL, out, POS, lane0, False, (g,))
            return carry

        lax.fori_loop(0, NB, step, 0)

    def mix(zero, first, second, data, out, b):
        lane0 = pl.multiple_of(b * EB, EB)
        lanes = pl.ds(lane0, EB)
        for m, r0, n in ((zero, 0, 768), (first, 768, 1024), (second, 1792, 512)):
            right = data[pl.ds(r0, n), lanes]
            for i in range(n // C):
                X[pl.ds(r0 + i * C, C), :] = nn(m[pl.ds(i * C, C), :], right)
        rotate(wide, X, POS, out, NATURAL, lane0, True)

    def backward(lo, hi):
        lax.fori_loop(lo, hi, lambda b, t: (mix(w0, M1b, M2b, hT, bT, b), t)[1], 0)

    def forward(lo, hi):
        lax.fori_loop(lo, hi, lambda b, t: (mix(W0T, M1f, M2f, yT, yT, b), t)[1], 0)

    gather(cotT, oh_t, hT, (0, 1, 2))
    backward(0, 1)

    def table(i, coefs):
        for copy in halo[i]:
            copy.wait_recv()
        for c in coefs:
            rows = pl.ds(c * A, A)
            both = jnp.concatenate([T3[0, rows, :], coef[rows, :], T3[1, rows, :]], axis=0)
            CT[pl.ds(c * C, C), :] = nt(one, both).astype(BF16)

    def put(tile, value):
        for k in range(2):
            G[pl.ds(k * HALF + tile * C, C), :] = value[:, k * 128 : (k + 1) * 128].astype(BF16)

    def zero_tiles(tile, i):
        for j in range(3):
            put(tile + j, nt(yT[pl.ds(i * C, C), :], hT[pl.ds(j * C, C), :]))

    def pair_tiles(tile, a0, b0, n, i):
        ya, yb = yT[pl.ds(a0 + i * C, C), :], yT[pl.ds(b0 + i * C, C), :]
        for j in range(n):
            ha, hb = hT[pl.ds(a0 + j * C, C), :], hT[pl.ds(b0 + j * C, C), :]
            put(tile + j, nt(ya, ha) + nt(yb, hb))
            put(tile + n + j, nt(ya, hb) - nt(yb, ha))

    table(0, range(4))
    gather(CT, oh_s, yT, (0, 1))
    zero_tiles(0, 0)
    zero_tiles(3, 1)
    swap[0].start()
    pair_tiles(6, 768, 1280, 2, 0)
    table(1, range(4, 9))
    gather(CT, oh_s, yT, (2,))
    advance(0, 0)
    zero_tiles(10, 2)
    swap[1].start()
    pair_tiles(13, 768, 1280, 2, 1)
    pair_tiles(17, 1792, 2048, 1, 0)
    swap[2].start()
    advance(0, 1)
    backward(1, 2)
    advance(0, 2)
    advance(1, 0)
    backward(2, 4)
    advance(1, 1)

    def sum_back(coefs):
        for c in coefs:
            total = nt(oh_s[...], bT[pl.ds(c * C, C), :])
            rows = pl.ds(c * A, A)
            SB[0, rows, :] = total[0:A].astype(BF16)
            SB[1, rows, :] = total[2 * A : 3 * A].astype(BF16)
            own_sum[rows, :] = total[A : 2 * A]

    sum_back(range(3))
    advance(2, 0)
    advance(1, 2)
    for copy in give[0]:
        copy.start()
    sum_back(range(3, 6))
    forward(0, 1)
    advance(2, 1)
    advance(3, 0)
    for copy in give[1]:
        copy.start()
    sum_back(range(6, 9))
    advance(2, 2)
    for copy in give[2]:
        copy.start()
    forward(1, 2)
    forward(2, 3)
    advance(3, 1)
    advance(4, 0)
    forward(3, 4)
    advance(3, 2)
    advance(4, 1)
    for c in range(NC):
        rows = pl.ds(c * A, A)
        total = nt(oh_t[...], yT[pl.ds(c * C, C), :])
        upd[rows, :] = (coef[rows, :].astype(F32) + total).astype(BF16)
    stores[6].start()
    advance(4, 2)
    for pair in give:
        for copy in pair:
            copy.wait_recv()
    gco[...] = (
        (cot[...].astype(F32) + own_sum[...]) + (RB[0].astype(F32) + RB[1].astype(F32))
    ).astype(BF16)
    stores[7].start()
    for p in range(3):
        advance(5, p)
    for p in range(3):
        for copy in share[p]:
            copy.wait_recv()
        stores[3 + p].start()
    for group in (*halo, *give, swap, *share, *(part for stage in stages for part in stage)):
        for copy in group:
            copy.wait_send()
    for copy in stores:
        copy.wait()


RUNS = ((0, 3, 0, 0), (3, 3, 0, 1), (6, 4, 1, 0), (10, 3, 0, 2), (13, 4, 1, 1), (17, 2, 2, 0))


def finish(upd, gco, O, upd_out, gco_out, g_zero, g_one, g_two, near, zero, one, two, sem):
    count = len(RUNS)
    straight = [
        pltpu.make_async_copy(upd, upd_out, sem.at[3 * count]),
        pltpu.make_async_copy(gco, gco_out, sem.at[3 * count + 1]),
    ]
    reads = []
    for i, (t, n, _, _) in enumerate(RUNS):
        rows = pl.ds(t * C, n * C)
        reads.append(pltpu.make_async_copy(O.at[:, rows], near.at[:, rows], sem.at[i]))
    for copy in reads + straight:
        copy.start()
    writes = []
    for i, (t, n, kind, row) in enumerate(RUNS):
        reads[i].wait()
        rows = pl.ds(row * C, C)
        parts = ((zero, g_zero),) if kind == 0 else ((one, g_one), (two, g_two))[kind - 1 : kind]
        held, far = parts[0]
        for part in range(1 if kind == 0 else 2):
            block = held if kind == 0 else held.at[part]
            width = n if kind == 0 else n // 2
            for j in range(width):
                for k in range(2):
                    block[rows, pl.ds(j * C + k * 128, 128)] = near[
                        k, pl.ds((t + part * width + j) * C, C), :
                    ].astype(F32)
            write = pltpu.make_async_copy(
                block.at[rows],
                (far if kind == 0 else far.at[part]).at[rows],
                sem.at[count + 2 * i + part],
            )
            write.start()
            writes.append(write)
    for copy in straight + writes:
        copy.wait()


def vmem(*shape):
    return pltpu.VMEM(shape, BF16)


def work(coef, cot, w0, w1, w2, rot, src, tgt, gate, live):
    whole = pl.BlockSpec(memory_space=pltpu.VMEM)
    far = pl.BlockSpec(memory_space=pltpu.HBM)
    return pl.pallas_call(
        body,
        out_shape=(
            jax.ShapeDtypeStruct((NC * A, C), BF16),
            jax.ShapeDtypeStruct((NC * A, C), BF16),
            jax.ShapeDtypeStruct((ROWS, 128), BF16),
        ),
        in_specs=[far] * 6 + [whole] * 3 + [pl.BlockSpec(memory_space=pltpu.SMEM)],
        out_specs=(far,) * 3,
        scratch_shapes=[
            vmem(NC * A, C),
            vmem(NC * A, C),
            vmem(ROT, E),
            vmem(NC * A, C),
            vmem(NC * A, C),
            vmem(ROWS, 128),
            vmem(768, 768),
            vmem(2, 512, 512),
            vmem(2, 256, 256),
            vmem(W9, E),
            vmem(W9, E),
            vmem(W9, E),
            pltpu.VMEM((W9, EB), F32),
            pltpu.VMEM((NC * A, C), F32),
            vmem(2, NC * A, C),
            vmem(W9, 3 * A),
            vmem(W9, A),
            vmem(768, 768),
            vmem(1024, 1024),
            vmem(1024, 1024),
            vmem(512, 512),
            vmem(512, 512),
            pltpu.VMEM((ROT, 8, E), F32),
            vmem(3 * A, E),
            vmem(A, E),
            vmem(ROWS, 128),
            vmem(HALF, 128),
            vmem(HALF, 128),
            vmem(3, HALF // 4, 128),
            pltpu.VMEM((HALF // 4, 128), F32),
            pltpu.VMEM((3, HALF // 16, 128), F32),
            pltpu.VMEM((HALF // 16, 128), F32),
            pltpu.VMEM((3, HALF // 16, 128), F32),
            vmem(2, NC * A, C),
            vmem(2, NC * A, C),
            pltpu.SemaphoreType.DMA((2, 5)),
            pltpu.SemaphoreType.DMA((2, 5)),
            pltpu.SemaphoreType.DMA((5, 3)),
            pltpu.SemaphoreType.DMA((5, 3)),
            pltpu.SemaphoreType.DMA((5, 3, 3)),
            pltpu.SemaphoreType.DMA((5, 3, 3)),
            pltpu.SemaphoreType.DMA((6,)),
            pltpu.SemaphoreType.DMA((8,)),
        ],
        compiler_params=pltpu.CompilerParams(
            collective_id=0, has_side_effects=True, vmem_limit_bytes=56 * 2**20
        ),
        name="layer",
    )(coef, cot, w0, w1, w2, rot, src, tgt, gate, live)


def shards(coeffs, cotangent, w_zero, w_one, w_two, source, target, rotation, gate, tile_live):
    def by_coef(rows):
        return jnp.transpose(rows[0], (1, 0, 2)).reshape(NC * A, C)

    def by_atom(rows):
        return jnp.transpose(rows.reshape(NC, A, C), (1, 0, 2))[None]

    upd, gco, grads = work(
        by_coef(coeffs), by_coef(cotangent), w_zero, w_one, w_two,
        rotation[0], source, target, gate, tile_live,
    )
    far = pl.BlockSpec(memory_space=pltpu.HBM)
    upd, gco, zero, one, two = pl.pallas_call(
        finish,
        out_shape=(
            jax.ShapeDtypeStruct((NC * A, C), BF16),
            jax.ShapeDtypeStruct((NC * A, C), BF16),
            jax.ShapeDtypeStruct((768, 768), F32),
            jax.ShapeDtypeStruct((2, 512, 512), F32),
            jax.ShapeDtypeStruct((2, 256, 256), F32),
        ),
        in_specs=[far] * 3,
        out_specs=(far,) * 5,
        scratch_shapes=[
            vmem(2, HALF, 128),
            pltpu.VMEM((768, 768), F32),
            pltpu.VMEM((2, 512, 512), F32),
            pltpu.VMEM((2, 256, 256), F32),
            pltpu.SemaphoreType.DMA((3 * len(RUNS) + 2,)),
        ],
        compiler_params=pltpu.CompilerParams(vmem_limit_bytes=62 * 2**20),
        name="finish",
    )(upd, gco, grads.reshape(2, HALF, 128))
    return by_atom(upd), by_atom(gco), zero, one, two


def solution(mesh):
    return jax.shard_map(
        shards,
        mesh=mesh,
        in_specs=(
            P("dp", "help", None, None),
            P("dp", "help", None, None),
            P(),
            P(),
            P(),
            P("dp", "help"),
            P("dp", "help"),
            P("dp", None, "help"),
            P("dp", "help"),
            P("dp", "help"),
        ),
        out_specs=(P("dp", "help", None, None), P("dp", "help", None, None), P(), P(), P()),
        check_vma=False,
    )
```

```python
import jax
import jax.numpy as jnp
from jax import lax
from jax.experimental import pallas as pl
from jax.experimental.pallas import tpu as pltpu
from jax.sharding import PartitionSpec as P

MESH = pl.DeviceIdType.MESH
F32 = jnp.float32
BF16 = jnp.bfloat16

A = 64
NC = 9
C = 256
E = 1024
EB = 256
NB = E // EB
ROT = 35
TILE = 64
W9 = NC * C
ROWS = 9728
HALF = ROWS // 2
BLOCKS = ((0, 1, 0), (1, 3, 1), (10, 5, 4))
ORDER = (0, 2, 6, 3, 7, 1, 5, 8, 4)
POS = tuple(ORDER.index(c) for c in range(NC))
NATURAL = tuple(range(NC))
UNITS = (6, 7, 6)
START = (0, 1536, 3328)
AXES = (("x", "y", "z"), ("y", "z", "x"), ("z", "x", "y"))


def nn(a, b):
    return jnp.dot(a, b, preferred_element_type=F32)


def nt(a, b):
    return lax.dot_general(a, b, (((1,), (1,)), ((), ())), preferred_element_type=F32)


def eye(n):
    r = lax.broadcasted_iota(jnp.int32, (n, n), 0)
    c = lax.broadcasted_iota(jnp.int32, (n, n), 1)
    return jnp.where(r == c, 1.0, 0.0).astype(BF16)


def rotate(wide, work, in_pos, out, out_pos, lane0, inverse, degrees=(0, 1, 2)):
    for lt in range(EB // 128):
        lanes = pl.ds(lane0 + lt * 128, 128)
        for offset, extent, first in [BLOCKS[g] for g in degrees]:
            d = [wide[offset + i, :, lanes][None] for i in range(extent * extent)]
            for chunk in range(0, C, 32):
                x = [
                    work[
                        pl.ds(in_pos[first + j] * C + chunk, 32), pl.ds(lt * 128, 128)
                    ].reshape(4, 8, 128)
                    for j in range(extent)
                ]
                for k in range(extent):
                    total = None
                    for j in range(extent):
                        entry = j * extent + k if inverse else k * extent + j
                        term = d[entry] * x[j]
                        total = term if total is None else total + term
                    out[pl.ds(out_pos[first + k] * C + chunk, 32), lanes] = total.reshape(
                        32, 128
                    ).astype(BF16)


def body(
    coef_in, cot_in, w0_in, w1_in, w2_in, rot_in, src, tgt, gate, live,
    upd_out, gco_out, O_out,
    coef, cot, rot, upd, gco, O, w0, w1, w2, hT, yT, bT, X, own_sum, T3, CT, cotT, W0T, M1f, M1b, M2f, M2b, wide, oh_s, oh_t,
    G, R0, S, R1, T1, R2, T2, R3, SB, RB,
    halo_s, halo_r, core_s, core_r, ring_s, ring_r, load_sem, store_sem,
):
    dp = lax.axis_index("dp")
    hp = lax.axis_index("help")
    x, core = dp // 2, dp % 2
    y, z = hp // 4, hp % 4
    at = {"x": x, "y": y, "z": z}

    def peer(axis, d):
        if axis == "x":
            return ((x + d) % 4 * 2 + core, hp)
        if axis == "y":
            return (dp, (y + d) % 4 * 4 + z)
        return (dp, y * 4 + (z + d) % 4)

    partner = (x * 2 + 1 - core, hp)
    above = (dp, (hp + 1) % 16)
    below = (dp, (hp + 15) % 16)

    barrier = pltpu.get_barrier_semaphore()
    peers = [partner, above, below] + [peer(a, d) for a in "xyz" for d in (1, 2, 3)]
    for device in peers:
        pl.semaphore_signal(barrier, inc=1, device_id=device, device_id_type=MESH)

    def remote(s, t, sem_s, sem_r, device):
        return pltpu.make_async_remote_copy(
            src_ref=s, dst_ref=t, send_sem=sem_s, recv_sem=sem_r,
            device_id=device, device_id_type=MESH,
        )

    halo = [
        [
            remote(coef_in.at[rows], T3.at[0, rows], halo_s.at[0, i], halo_r.at[0, i], above),
            remote(coef_in.at[rows], T3.at[1, rows], halo_s.at[1, i], halo_r.at[1, i], below),
        ]
        for i, rows in enumerate((pl.ds(0, 4 * A), pl.ds(4 * A, 5 * A)))
    ]
    give = [
        [
            remote(SB.at[1, rows], RB.at[0, rows], halo_s.at[0, i], halo_r.at[0, i], above),
            remote(SB.at[0, rows], RB.at[1, rows], halo_s.at[1, i], halo_r.at[1, i], below),
        ]
        for i, rows in ((2 + i, pl.ds(3 * A * i, 3 * A)) for i in range(3))
    ]
    loads = [
        pltpu.make_async_copy(far, near, load_sem.at[i])
        for i, (far, near) in enumerate(
            ((cot_in, cot), (rot_in, rot), (coef_in, coef), (w0_in, w0), (w1_in, w1), (w2_in, w2))
        )
    ]
    for copy in loads:
        copy.start()

    def stored(half, p):
        rows = pl.ds(pl.multiple_of(half * HALF + START[p], 256), UNITS[p] * 256)
        return O.at[rows], O_out.at[rows]

    stores = [
        pltpu.make_async_copy(*pair, store_sem.at[i])
        for i, pair in enumerate(
            [stored(core, p) for p in range(3)]
            + [stored(1 - core, p) for p in range(3)]
            + [(upd, upd_out), (gco, gco_out)]
        )
    ]

    swap = [
        remote(
            G.at[pl.ds(pl.multiple_of((1 - core) * HALF + START[p], 256), UNITS[p] * 256)],
            R0.at[pl.ds(START[p], UNITS[p] * 256)],
            core_s.at[4, p], core_r.at[4, p], partner,
        )
        for p in range(3)
    ]

    def quarter(p, d):
        n = UNITS[p] * 64
        row = core * HALF + START[p] + (at[AXES[p][0]] + 4 - d) % 4 * n
        return O.at[pl.ds(pl.multiple_of(row, 64), n)]

    share = [
        [
            remote(quarter(p, d), quarter(p, d), core_s.at[d, p], core_r.at[d, p], partner)
            for d in range(4)
        ]
        for p in range(3)
    ]

    def ring(stage, make):
        return [
            [
                remote(*make(p, d), ring_s.at[stage, p, d - 1], ring_r.at[stage, p, d - 1], peer(AXES[p][(0, 1, 2, 1, 0)[stage]], d))
                for d in (1, 2, 3)
            ]
            for p in range(3)
        ]

    def first_make(p, d):
        q = UNITS[p] * 64
        j = (at[AXES[p][0]] + d) % 4
        return (
            S.at[pl.ds(pl.multiple_of(START[p] + j * q, 64), q)],
            R1.at[d - 1, pl.ds(START[p] // 4, q)],
        )

    def second_make(p, d):
        q = UNITS[p] * 16
        j = (at[AXES[p][1]] + d) % 4
        return (
            T1.at[pl.ds(pl.multiple_of(START[p] // 4 + j * q, 16), q)],
            R2.at[d - 1, pl.ds(START[p] // 16, q)],
        )

    def third_make(p, d):
        rows = pl.ds(START[p] // 16, UNITS[p] * 16)
        return T2.at[rows], R3.at[d - 1, rows]

    def place(p, deep):
        q = UNITS[p] * 16
        base = core * HALF + START[p] + at[AXES[p][0]] * (4 * q)
        if deep:
            return pl.ds(pl.multiple_of(base + at[AXES[p][1]] * q, 16), q)
        return pl.ds(pl.multiple_of(base, 64), 4 * q)

    def fourth_make(p, d):
        return O.at[place(p, True)], O.at[place(p, True)]

    def fifth_make(p, d):
        return O.at[place(p, False)], O.at[place(p, False)]

    stages = [
        ring(i, m)
        for i, m in enumerate((first_make, second_make, third_make, fourth_make, fifth_make))
    ]

    def go(stage, p):
        for copy in stages[stage][p]:
            copy.start()

    def arrive(stage, p):
        for copy in stages[stage][p]:
            copy.wait_recv()

    def advance(k, p):
        n = UNITS[p] * 64
        if k == 0:
            swap[p].wait_recv()

            def add_core(i, carry):
                rows = pl.ds(pl.multiple_of(START[p] + i * n, 64), n)
                own = pl.ds(pl.multiple_of(core * HALF + START[p] + i * n, 64), n)
                S[rows, :] = (G[own, :].astype(F32) + R0[rows, :].astype(F32)).astype(BF16)
                return carry

            lax.fori_loop(0, 4, add_core, 0)
            go(0, p)
        elif k == 1:
            arrive(0, p)
            own = pl.ds(pl.multiple_of(START[p] + at[AXES[p][0]] * n, 64), n)
            rows = pl.ds(START[p] // 4, n)
            T1[rows, :] = (S[own, :].astype(F32) + R1[1, rows, :].astype(F32)) + (
                R1[0, rows, :].astype(F32) + R1[2, rows, :].astype(F32)
            )
            go(1, p)
        elif k == 2:
            arrive(1, p)
            n = n // 4
            own = pl.ds(pl.multiple_of(START[p] // 4 + at[AXES[p][1]] * n, 16), n)
            rows = pl.ds(START[p] // 16, n)
            T2[rows, :] = (T1[own, :] + R2[1, rows, :]) + (R2[0, rows, :] + R2[2, rows, :])
            go(2, p)
        elif k == 3:
            arrive(2, p)
            rows = pl.ds(START[p] // 16, n // 4)
            O[place(p, True), :] = (
                (T2[rows, :] + R3[1, rows, :]) + (R3[0, rows, :] + R3[2, rows, :])
            ).astype(BF16)
            go(3, p)
        elif k == 4:
            arrive(3, p)
            go(4, p)
            share[p][0].start()
        else:
            for d in (1, 2, 3):
                stages[4][p][d - 1].wait_recv()
                share[p][d].start()
            stores[p].start()

    pl.semaphore_wait(barrier, len(peers))
    for pair in halo:
        for copy in pair:
            copy.start()

    loads[0].wait()
    loads[1].wait()
    wide[...] = jnp.broadcast_to(rot[...].astype(F32)[:, None, :], (ROT, 8, E))
    lane = lax.broadcasted_iota(jnp.int32, (1, E), 1) // TILE
    alive = jnp.zeros((1, E), F32)
    for t in range(E // TILE):
        alive = jnp.where(lane == t, live[0, t].astype(F32), alive)
    q = gate[...].astype(F32) * alive
    for r in range(0, 3 * A, A):
        ids = lax.broadcasted_iota(jnp.int32, (A, E), 0)
        oh_s[pl.ds(r, A), :] = jnp.where(ids + r == src[...], 1.0, 0.0).astype(BF16)
    ids = lax.broadcasted_iota(jnp.int32, (A, E), 0)
    oh_t[...] = jnp.where(ids == tgt[...], q, 0.0).astype(BF16)

    one = eye(C)
    for c in range(NC):
        cotT[pl.ds(c * C, C), :] = nt(one, cot[pl.ds(c * A, A), :]).astype(BF16)
    for copy in loads[2:]:
        copy.wait()
    for i in range(3):
        W0T[pl.ds(i * C, C), :] = nt(one, w0[:, pl.ds(i * C, C)]).astype(BF16)
    for fwd, bwd, w, n in ((M1f, M1b, w1, 512), (M2f, M2b, w2, 256)):
        lo, hi = pl.ds(0, n), pl.ds(n, n)
        bwd[lo, lo] = w[0]
        bwd[lo, hi] = w[1]
        bwd[hi, lo] = -w[1]
        bwd[hi, hi] = w[0]
        for i in range(n // C):
            rows, next_rows = pl.ds(i * C, C), pl.ds(n + i * C, C)
            real = nt(one, w[0, :, pl.ds(i * C, C)])
            imag = nt(one, w[1, :, pl.ds(i * C, C)])
            fwd[rows, lo] = real.astype(BF16)
            fwd[rows, hi] = (-imag).astype(BF16)
            fwd[next_rows, lo] = imag.astype(BF16)
            fwd[next_rows, hi] = real.astype(BF16)

    def gather(table, onehot, out, degrees):
        def step(b, carry):
            lane0 = pl.multiple_of(b * EB, EB)
            pick = onehot[:, pl.ds(lane0, EB)]
            for g in degrees:
                for c in range(g * g, (g + 1) * (g + 1)):
                    X[pl.ds(c * C, C), :] = nn(table[pl.ds(c * C, C), :], pick)
                rotate(wide, X, NATURAL, out, POS, lane0, False, (g,))
            return carry

        lax.fori_loop(0, NB, step, 0)

    def mix(zero, first, second, data, out, b):
        lane0 = pl.multiple_of(b * EB, EB)
        lanes = pl.ds(lane0, EB)
        for m, r0, n in ((zero, 0, 768), (first, 768, 1024), (second, 1792, 512)):
            right = data[pl.ds(r0, n), lanes]
            for i in range(n // C):
                X[pl.ds(r0 + i * C, C), :] = nn(m[pl.ds(i * C, C), :], right)
        rotate(wide, X, POS, out, NATURAL, lane0, True)

    def backward(lo, hi):
        lax.fori_loop(lo, hi, lambda b, t: (mix(w0, M1b, M2b, hT, bT, b), t)[1], 0)

    def forward(lo, hi):
        lax.fori_loop(lo, hi, lambda b, t: (mix(W0T, M1f, M2f, yT, yT, b), t)[1], 0)

    gather(cotT, oh_t, hT, (0, 1, 2))
    backward(0, 1)

    def table(i, coefs):
        for copy in halo[i]:
            copy.wait_recv()
        for c in coefs:
            rows = pl.ds(c * A, A)
            both = jnp.concatenate([T3[0, rows, :], coef[rows, :], T3[1, rows, :]], axis=0)
            CT[pl.ds(c * C, C), :] = nt(one, both).astype(BF16)

    def put(tile, value):
        for k in range(2):
            G[pl.ds(k * HALF + tile * C, C), :] = value[:, k * 128 : (k + 1) * 128].astype(BF16)

    def zero_tiles(tile, i):
        for j in range(3):
            put(tile + j, nt(yT[pl.ds(i * C, C), :], hT[pl.ds(j * C, C), :]))

    def pair_tiles(tile, a0, b0, n, i):
        ya, yb = yT[pl.ds(a0 + i * C, C), :], yT[pl.ds(b0 + i * C, C), :]
        for j in range(n):
            ha, hb = hT[pl.ds(a0 + j * C, C), :], hT[pl.ds(b0 + j * C, C), :]
            put(tile + j, nt(ya, ha) + nt(yb, hb))
            put(tile + n + j, nt(ya, hb) - nt(yb, ha))

    table(0, range(4))
    gather(CT, oh_s, yT, (0, 1))
    zero_tiles(0, 0)
    zero_tiles(3, 1)
    swap[0].start()
    pair_tiles(6, 768, 1280, 2, 0)
    table(1, range(4, 9))
    gather(CT, oh_s, yT, (2,))
    advance(0, 0)
    zero_tiles(10, 2)
    swap[1].start()
    pair_tiles(13, 768, 1280, 2, 1)
    pair_tiles(17, 1792, 2048, 1, 0)
    swap[2].start()
    advance(0, 1)
    backward(1, 2)
    advance(0, 2)
    advance(1, 0)
    backward(2, 4)
    advance(1, 1)

    def sum_back(coefs):
        for c in coefs:
            total = nt(oh_s[...], bT[pl.ds(c * C, C), :])
            rows = pl.ds(c * A, A)
            SB[0, rows, :] = total[0:A].astype(BF16)
            SB[1, rows, :] = total[2 * A : 3 * A].astype(BF16)
            own_sum[rows, :] = total[A : 2 * A]

    sum_back(range(3))
    advance(2, 0)
    advance(1, 2)
    for copy in give[0]:
        copy.start()
    sum_back(range(3, 6))
    forward(0, 1)
    advance(2, 1)
    advance(3, 0)
    for copy in give[1]:
        copy.start()
    sum_back(range(6, 9))
    advance(2, 2)
    for copy in give[2]:
        copy.start()
    forward(1, 2)
    forward(2, 3)
    advance(3, 1)
    advance(4, 0)
    forward(3, 4)
    advance(3, 2)
    advance(4, 1)
    for c in range(NC):
        rows = pl.ds(c * A, A)
        total = nt(oh_t[...], yT[pl.ds(c * C, C), :])
        upd[rows, :] = (coef[rows, :].astype(F32) + total).astype(BF16)
    stores[6].start()
    advance(4, 2)
    for pair in give:
        for copy in pair:
            copy.wait_recv()
    gco[...] = (
        (cot[...].astype(F32) + own_sum[...]) + (RB[0].astype(F32) + RB[1].astype(F32))
    ).astype(BF16)
    stores[7].start()
    for p in range(3):
        advance(5, p)
    for p in range(3):
        for copy in share[p]:
            copy.wait_recv()
        stores[3 + p].start()
    for group in (*halo, *give, swap, *share, *(part for stage in stages for part in stage)):
        for copy in group:
            copy.wait_send()
    for copy in stores:
        copy.wait()


RUNS = ((0, 3, 0, 0), (3, 3, 0, 1), (6, 4, 1, 0), (10, 3, 0, 2), (13, 4, 1, 1), (17, 2, 2, 0))


def finish(upd, gco, O, upd_out, gco_out, g_zero, g_one, g_two, near, rows_near, zero, one, two, sem):
    count = len(RUNS)
    through = [
        [
            pltpu.make_async_copy(start, rows_near.at[i], sem.at[3 * count + 2 * i]),
            pltpu.make_async_copy(rows_near.at[i], end, sem.at[3 * count + 2 * i + 1]),
        ]
        for i, (start, end) in enumerate(((upd, upd_out), (gco, gco_out)))
    ]
    reads = []
    for i, (t, n, _, _) in enumerate(RUNS):
        rows = pl.ds(t * C, n * C)
        reads.append(pltpu.make_async_copy(O.at[:, rows], near.at[:, rows], sem.at[i]))
    for copy in reads + [inward for inward, _ in through]:
        copy.start()
    writes = []
    for i, (t, n, kind, row) in enumerate(RUNS):
        reads[i].wait()
        rows = pl.ds(row * C, C)
        parts = ((zero, g_zero),) if kind == 0 else ((one, g_one), (two, g_two))[kind - 1 : kind]
        held, far = parts[0]
        for part in range(1 if kind == 0 else 2):
            block = held if kind == 0 else held.at[part]
            width = n if kind == 0 else n // 2
            for j in range(width):
                for k in range(2):
                    block[rows, pl.ds(j * C + k * 128, 128)] = near[
                        k, pl.ds((t + part * width + j) * C, C), :
                    ].astype(F32)
            write = pltpu.make_async_copy(
                block.at[rows],
                (far if kind == 0 else far.at[part]).at[rows],
                sem.at[count + 2 * i + part],
            )
            write.start()
            writes.append(write)
    for inward, outward in through:
        inward.wait()
        outward.start()
        writes.append(outward)
    for copy in writes:
        copy.wait()


def vmem(*shape):
    return pltpu.VMEM(shape, BF16)


def work(coef, cot, w0, w1, w2, rot, src, tgt, gate, live):
    whole = pl.BlockSpec(memory_space=pltpu.VMEM)
    far = pl.BlockSpec(memory_space=pltpu.HBM)
    return pl.pallas_call(
        body,
        out_shape=(
            jax.ShapeDtypeStruct((NC * A, C), BF16),
            jax.ShapeDtypeStruct((NC * A, C), BF16),
            jax.ShapeDtypeStruct((ROWS, 128), BF16),
        ),
        in_specs=[far] * 6 + [whole] * 3 + [pl.BlockSpec(memory_space=pltpu.SMEM)],
        out_specs=(far,) * 3,
        scratch_shapes=[
            vmem(NC * A, C),
            vmem(NC * A, C),
            vmem(ROT, E),
            vmem(NC * A, C),
            vmem(NC * A, C),
            vmem(ROWS, 128),
            vmem(768, 768),
            vmem(2, 512, 512),
            vmem(2, 256, 256),
            vmem(W9, E),
            vmem(W9, E),
            vmem(W9, E),
            pltpu.VMEM((W9, EB), F32),
            pltpu.VMEM((NC * A, C), F32),
            vmem(2, NC * A, C),
            vmem(W9, 3 * A),
            vmem(W9, A),
            vmem(768, 768),
            vmem(1024, 1024),
            vmem(1024, 1024),
            vmem(512, 512),
            vmem(512, 512),
            pltpu.VMEM((ROT, 8, E), F32),
            vmem(3 * A, E),
            vmem(A, E),
            vmem(ROWS, 128),
            vmem(HALF, 128),
            vmem(HALF, 128),
            vmem(3, HALF // 4, 128),
            pltpu.VMEM((HALF // 4, 128), F32),
            pltpu.VMEM((3, HALF // 16, 128), F32),
            pltpu.VMEM((HALF // 16, 128), F32),
            pltpu.VMEM((3, HALF // 16, 128), F32),
            vmem(2, NC * A, C),
            vmem(2, NC * A, C),
            pltpu.SemaphoreType.DMA((2, 5)),
            pltpu.SemaphoreType.DMA((2, 5)),
            pltpu.SemaphoreType.DMA((5, 3)),
            pltpu.SemaphoreType.DMA((5, 3)),
            pltpu.SemaphoreType.DMA((5, 3, 3)),
            pltpu.SemaphoreType.DMA((5, 3, 3)),
            pltpu.SemaphoreType.DMA((6,)),
            pltpu.SemaphoreType.DMA((8,)),
        ],
        compiler_params=pltpu.CompilerParams(
            collective_id=0, has_side_effects=True, vmem_limit_bytes=56 * 2**20
        ),
        name="layer",
    )(coef, cot, w0, w1, w2, rot, src, tgt, gate, live)


def shards(coeffs, cotangent, w_zero, w_one, w_two, source, target, rotation, gate, tile_live):
    def by_coef(rows):
        return jnp.transpose(rows[0], (1, 0, 2)).reshape(NC * A, C)

    def by_atom(rows):
        return jnp.transpose(rows.reshape(NC, A, C), (1, 0, 2))[None]

    upd, gco, grads = work(
        by_coef(coeffs), by_coef(cotangent), w_zero, w_one, w_two,
        rotation[0], source, target, gate, tile_live,
    )
    far = pl.BlockSpec(memory_space=pltpu.HBM)
    upd, gco, zero, one, two = pl.pallas_call(
        finish,
        out_shape=(
            jax.ShapeDtypeStruct((NC * A, C), BF16),
            jax.ShapeDtypeStruct((NC * A, C), BF16),
            jax.ShapeDtypeStruct((768, 768), F32),
            jax.ShapeDtypeStruct((2, 512, 512), F32),
            jax.ShapeDtypeStruct((2, 256, 256), F32),
        ),
        in_specs=[far] * 3,
        out_specs=(far,) * 5,
        scratch_shapes=[
            vmem(2, HALF, 128),
            vmem(2, NC * A, C),
            pltpu.VMEM((768, 768), F32),
            pltpu.VMEM((2, 512, 512), F32),
            pltpu.VMEM((2, 256, 256), F32),
            pltpu.SemaphoreType.DMA((3 * len(RUNS) + 4,)),
        ],
        compiler_params=pltpu.CompilerParams(vmem_limit_bytes=62 * 2**20),
        name="finish",
    )(upd, gco, grads.reshape(2, HALF, 128))
    return by_atom(upd), by_atom(gco), zero, one, two


def solution(mesh):
    return jax.shard_map(
        shards,
        mesh=mesh,
        in_specs=(
            P("dp", "help", None, None),
            P("dp", "help", None, None),
            P(),
            P(),
            P(),
            P("dp", "help"),
            P("dp", "help"),
            P("dp", None, "help"),
            P("dp", "help"),
            P("dp", "help"),
        ),
        out_specs=(P("dp", "help", None, None), P("dp", "help", None, None), P(), P(), P()),
        check_vma=False,
    )
```

```python
import jax
import jax.numpy as jnp
from jax import lax
from jax.experimental import pallas as pl
from jax.experimental.pallas import tpu as pltpu
from jax.sharding import PartitionSpec as P

MESH = pl.DeviceIdType.MESH
F32 = jnp.float32
BF16 = jnp.bfloat16

A = 64
NC = 9
C = 256
E = 1024
EB = 256
NB = E // EB
ROT = 35
TILE = 64
W9 = NC * C
ROWS = 9728
HALF = ROWS // 2
BLOCKS = ((0, 1, 0), (1, 3, 1), (10, 5, 4))
ORDER = (0, 2, 6, 3, 7, 1, 5, 8, 4)
POS = tuple(ORDER.index(c) for c in range(NC))
NATURAL = tuple(range(NC))
UNITS = (6, 7, 6)
START = (0, 1536, 3328)
AXES = (("x", "y", "z"), ("y", "z", "x"), ("z", "x", "y"))


def nn(a, b):
    return jnp.dot(a, b, preferred_element_type=F32)


def nt(a, b):
    return lax.dot_general(a, b, (((1,), (1,)), ((), ())), preferred_element_type=F32)


def eye(n):
    r = lax.broadcasted_iota(jnp.int32, (n, n), 0)
    c = lax.broadcasted_iota(jnp.int32, (n, n), 1)
    return jnp.where(r == c, 1.0, 0.0).astype(BF16)


def rotate(wide, work, in_pos, out, out_pos, lane0, inverse, degrees=(0, 1, 2)):
    for lt in range(EB // 128):
        lanes = pl.ds(lane0 + lt * 128, 128)
        for offset, extent, first in [BLOCKS[g] for g in degrees]:
            d = [wide[offset + i, :, lanes][None] for i in range(extent * extent)]
            for chunk in range(0, C, 32):
                x = [
                    work[
                        pl.ds(in_pos[first + j] * C + chunk, 32), pl.ds(lt * 128, 128)
                    ].reshape(4, 8, 128)
                    for j in range(extent)
                ]
                for k in range(extent):
                    total = None
                    for j in range(extent):
                        entry = j * extent + k if inverse else k * extent + j
                        term = d[entry] * x[j]
                        total = term if total is None else total + term
                    out[pl.ds(out_pos[first + k] * C + chunk, 32), lanes] = total.reshape(
                        32, 128
                    ).astype(BF16)


def body(
    coef_in, cot_in, w0_in, w1_in, w2_in, rot_in, src, tgt, gate, live,
    upd_out, gco_out, O_out,
    coef, cot, rot, upd, gco, O, w0, w1, w2, hT, yT, bT, X, own_sum, T3, CT, cotT, W0T, M1f, M1b, M2f, M2b, wide, oh_s, oh_t,
    G, R0, S, R1, T1, R2, T2, R3, SB, RB,
    halo_s, halo_r, core_s, core_r, ring_s, ring_r, load_sem, store_sem,
):
    dp = lax.axis_index("dp")
    hp = lax.axis_index("help")
    x, core = dp // 2, dp % 2
    y, z = hp // 4, hp % 4
    at = {"x": x, "y": y, "z": z}

    def peer(axis, d):
        if axis == "x":
            return ((x + d) % 4 * 2 + core, hp)
        if axis == "y":
            return (dp, (y + d) % 4 * 4 + z)
        return (dp, y * 4 + (z + d) % 4)

    partner = (x * 2 + 1 - core, hp)
    above = (dp, (hp + 1) % 16)
    below = (dp, (hp + 15) % 16)

    barrier = pltpu.get_barrier_semaphore()
    peers = [partner, above, below] + [peer(a, d) for a in "xyz" for d in (1, 2, 3)]
    for device in peers:
        pl.semaphore_signal(barrier, inc=1, device_id=device, device_id_type=MESH)

    def remote(s, t, sem_s, sem_r, device):
        return pltpu.make_async_remote_copy(
            src_ref=s, dst_ref=t, send_sem=sem_s, recv_sem=sem_r,
            device_id=device, device_id_type=MESH,
        )

    halo = [
        [
            remote(coef_in.at[rows], T3.at[0, rows], halo_s.at[0, i], halo_r.at[0, i], above),
            remote(coef_in.at[rows], T3.at[1, rows], halo_s.at[1, i], halo_r.at[1, i], below),
        ]
        for i, rows in enumerate((pl.ds(0, 4 * A), pl.ds(4 * A, 5 * A)))
    ]
    give = [
        [
            remote(SB.at[1, rows], RB.at[0, rows], halo_s.at[0, i], halo_r.at[0, i], above),
            remote(SB.at[0, rows], RB.at[1, rows], halo_s.at[1, i], halo_r.at[1, i], below),
        ]
        for i, rows in ((2 + i, pl.ds(3 * A * i, 3 * A)) for i in range(3))
    ]
    loads = [
        pltpu.make_async_copy(far, near, load_sem.at[i])
        for i, (far, near) in enumerate(
            ((cot_in, cot), (rot_in, rot), (coef_in, coef), (w0_in, w0), (w1_in, w1), (w2_in, w2))
        )
    ]
    for copy in loads:
        copy.start()

    def stored(half, p):
        rows = pl.ds(pl.multiple_of(half * HALF + START[p], 256), UNITS[p] * 256)
        return O.at[rows], O_out.at[rows]

    stores = [
        pltpu.make_async_copy(*pair, store_sem.at[i])
        for i, pair in enumerate(
            [stored(core, p) for p in range(3)]
            + [stored(1 - core, p) for p in range(3)]
            + [(upd, upd_out), (gco, gco_out)]
        )
    ]

    swap = [
        remote(
            G.at[pl.ds(pl.multiple_of((1 - core) * HALF + START[p], 256), UNITS[p] * 256)],
            R0.at[pl.ds(START[p], UNITS[p] * 256)],
            core_s.at[4, p], core_r.at[4, p], partner,
        )
        for p in range(3)
    ]

    def quarter(p, d):
        n = UNITS[p] * 64
        row = core * HALF + START[p] + (at[AXES[p][0]] + 4 - d) % 4 * n
        return O.at[pl.ds(pl.multiple_of(row, 64), n)]

    share = [
        [
            remote(quarter(p, d), quarter(p, d), core_s.at[d, p], core_r.at[d, p], partner)
            for d in range(4)
        ]
        for p in range(3)
    ]

    def ring(stage, make):
        return [
            [
                remote(*make(p, d), ring_s.at[stage, p, d - 1], ring_r.at[stage, p, d - 1], peer(AXES[p][(0, 1, 2, 1, 0)[stage]], d))
                for d in (1, 2, 3)
            ]
            for p in range(3)
        ]

    def first_make(p, d):
        q = UNITS[p] * 64
        j = (at[AXES[p][0]] + d) % 4
        return (
            S.at[pl.ds(pl.multiple_of(START[p] + j * q, 64), q)],
            R1.at[d - 1, pl.ds(START[p] // 4, q)],
        )

    def second_make(p, d):
        q = UNITS[p] * 16
        j = (at[AXES[p][1]] + d) % 4
        return (
            T1.at[pl.ds(pl.multiple_of(START[p] // 4 + j * q, 16), q)],
            R2.at[d - 1, pl.ds(START[p] // 16, q)],
        )

    def third_make(p, d):
        rows = pl.ds(START[p] // 16, UNITS[p] * 16)
        return T2.at[rows], R3.at[d - 1, rows]

    def place(p, deep):
        q = UNITS[p] * 16
        base = core * HALF + START[p] + at[AXES[p][0]] * (4 * q)
        if deep:
            return pl.ds(pl.multiple_of(base + at[AXES[p][1]] * q, 16), q)
        return pl.ds(pl.multiple_of(base, 64), 4 * q)

    def fourth_make(p, d):
        return O.at[place(p, True)], O.at[place(p, True)]

    def fifth_make(p, d):
        return O.at[place(p, False)], O.at[place(p, False)]

    stages = [
        ring(i, m)
        for i, m in enumerate((first_make, second_make, third_make, fourth_make, fifth_make))
    ]

    def go(stage, p):
        for copy in stages[stage][p]:
            copy.start()

    def arrive(stage, p):
        for copy in stages[stage][p]:
            copy.wait_recv()

    def advance(k, p):
        n = UNITS[p] * 64
        if k == 0:
            swap[p].wait_recv()

            def add_core(i, carry):
                rows = pl.ds(pl.multiple_of(START[p] + i * n, 64), n)
                own = pl.ds(pl.multiple_of(core * HALF + START[p] + i * n, 64), n)
                S[rows, :] = (G[own, :].astype(F32) + R0[rows, :].astype(F32)).astype(BF16)
                return carry

            lax.fori_loop(0, 4, add_core, 0)
            go(0, p)
        elif k == 1:
            arrive(0, p)
            own = pl.ds(pl.multiple_of(START[p] + at[AXES[p][0]] * n, 64), n)
            rows = pl.ds(START[p] // 4, n)
            T1[rows, :] = (S[own, :].astype(F32) + R1[1, rows, :].astype(F32)) + (
                R1[0, rows, :].astype(F32) + R1[2, rows, :].astype(F32)
            )
            go(1, p)
        elif k == 2:
            arrive(1, p)
            n = n // 4
            own = pl.ds(pl.multiple_of(START[p] // 4 + at[AXES[p][1]] * n, 16), n)
            rows = pl.ds(START[p] // 16, n)
            T2[rows, :] = (T1[own, :] + R2[1, rows, :]) + (R2[0, rows, :] + R2[2, rows, :])
            go(2, p)
        elif k == 3:
            arrive(2, p)
            rows = pl.ds(START[p] // 16, n // 4)
            O[place(p, True), :] = (
                (T2[rows, :] + R3[1, rows, :]) + (R3[0, rows, :] + R3[2, rows, :])
            ).astype(BF16)
            go(3, p)
        elif k == 4:
            arrive(3, p)
            go(4, p)
            share[p][0].start()
        else:
            for d in (1, 2, 3):
                stages[4][p][d - 1].wait_recv()
                share[p][d].start()
            stores[p].start()

    pl.semaphore_wait(barrier, len(peers))
    for pair in halo:
        for copy in pair:
            copy.start()

    loads[0].wait()
    loads[1].wait()
    wide[...] = jnp.broadcast_to(rot[...].astype(F32)[:, None, :], (ROT, 8, E))
    lane = lax.broadcasted_iota(jnp.int32, (1, E), 1) // TILE
    alive = jnp.zeros((1, E), F32)
    for t in range(E // TILE):
        alive = jnp.where(lane == t, live[0, t].astype(F32), alive)
    q = gate[...].astype(F32) * alive
    for r in range(0, 3 * A, A):
        ids = lax.broadcasted_iota(jnp.int32, (A, E), 0)
        oh_s[pl.ds(r, A), :] = jnp.where(ids + r == src[...], 1.0, 0.0).astype(BF16)
    ids = lax.broadcasted_iota(jnp.int32, (A, E), 0)
    oh_t[...] = jnp.where(ids == tgt[...], q, 0.0).astype(BF16)

    one = eye(C)
    for c in range(NC):
        cotT[pl.ds(c * C, C), :] = nt(one, cot[pl.ds(c * A, A), :]).astype(BF16)
    loads[2].wait()

    def gather(table, onehot, out, degrees):
        def step(b, carry):
            lane0 = pl.multiple_of(b * EB, EB)
            pick = onehot[:, pl.ds(lane0, EB)]
            for g in degrees:
                for c in range(g * g, (g + 1) * (g + 1)):
                    X[pl.ds(c * C, C), :] = nn(table[pl.ds(c * C, C), :], pick)
                rotate(wide, X, NATURAL, out, POS, lane0, False, (g,))
            return carry

        lax.fori_loop(0, NB, step, 0)

    def mix(zero, first, second, data, out, b):
        lane0 = pl.multiple_of(b * EB, EB)
        lanes = pl.ds(lane0, EB)
        for m, r0, n in ((zero, 0, 768), (first, 768, 1024), (second, 1792, 512)):
            right = data[pl.ds(r0, n), lanes]
            for i in range(n // C):
                X[pl.ds(r0 + i * C, C), :] = nn(m[pl.ds(i * C, C), :], right)
        rotate(wide, X, POS, out, NATURAL, lane0, True)

    def backward(lo, hi):
        lax.fori_loop(lo, hi, lambda b, t: (mix(w0, M1b, M2b, hT, bT, b), t)[1], 0)

    def forward(lo, hi):
        lax.fori_loop(lo, hi, lambda b, t: (mix(W0T, M1f, M2f, yT, yT, b), t)[1], 0)

    gather(cotT, oh_t, hT, (0, 1, 2))

    def table(i, coefs):
        for copy in halo[i]:
            copy.wait_recv()
        for c in coefs:
            rows = pl.ds(c * A, A)
            both = jnp.concatenate([T3[0, rows, :], coef[rows, :], T3[1, rows, :]], axis=0)
            CT[pl.ds(c * C, C), :] = nt(one, both).astype(BF16)

    def put(tile, value):
        for k in range(2):
            G[pl.ds(k * HALF + tile * C, C), :] = value[:, k * 128 : (k + 1) * 128].astype(BF16)

    def zero_tiles(tile, i):
        for j in range(3):
            put(tile + j, nt(yT[pl.ds(i * C, C), :], hT[pl.ds(j * C, C), :]))

    def pair_tiles(tile, a0, b0, n, i):
        ya, yb = yT[pl.ds(a0 + i * C, C), :], yT[pl.ds(b0 + i * C, C), :]
        for j in range(n):
            ha, hb = hT[pl.ds(a0 + j * C, C), :], hT[pl.ds(b0 + j * C, C), :]
            put(tile + j, nt(ya, ha) + nt(yb, hb))
            put(tile + n + j, nt(ya, hb) - nt(yb, ha))

    table(0, range(4))
    gather(CT, oh_s, yT, (0, 1))
    zero_tiles(0, 0)
    zero_tiles(3, 1)
    swap[0].start()
    pair_tiles(6, 768, 1280, 2, 0)
    table(1, range(4, 9))
    advance(0, 0)
    gather(CT, oh_s, yT, (2,))
    zero_tiles(10, 2)
    swap[1].start()
    pair_tiles(13, 768, 1280, 2, 1)
    pair_tiles(17, 1792, 2048, 1, 0)
    swap[2].start()
    advance(0, 1)
    for copy in loads[3:]:
        copy.wait()
    for i in range(3):
        W0T[pl.ds(i * C, C), :] = nt(one, w0[:, pl.ds(i * C, C)]).astype(BF16)
    for fwd, bwd, w, n in ((M1f, M1b, w1, 512), (M2f, M2b, w2, 256)):
        lo, hi = pl.ds(0, n), pl.ds(n, n)
        bwd[lo, lo] = w[0]
        bwd[lo, hi] = w[1]
        bwd[hi, lo] = -w[1]
        bwd[hi, hi] = w[0]
        for i in range(n // C):
            rows, next_rows = pl.ds(i * C, C), pl.ds(n + i * C, C)
            real = nt(one, w[0, :, pl.ds(i * C, C)])
            imag = nt(one, w[1, :, pl.ds(i * C, C)])
            fwd[rows, lo] = real.astype(BF16)
            fwd[rows, hi] = (-imag).astype(BF16)
            fwd[next_rows, lo] = imag.astype(BF16)
            fwd[next_rows, hi] = real.astype(BF16)
    backward(0, 1)
    advance(0, 2)
    advance(1, 0)
    backward(1, 4)
    advance(1, 1)

    def sum_back(coefs):
        for c in coefs:
            total = nt(oh_s[...], bT[pl.ds(c * C, C), :])
            rows = pl.ds(c * A, A)
            SB[0, rows, :] = total[0:A].astype(BF16)
            SB[1, rows, :] = total[2 * A : 3 * A].astype(BF16)
            own_sum[rows, :] = total[A : 2 * A]

    sum_back(range(3))
    advance(2, 0)
    advance(1, 2)
    for copy in give[0]:
        copy.start()
    sum_back(range(3, 6))
    forward(0, 1)
    advance(2, 1)
    advance(3, 0)
    for copy in give[1]:
        copy.start()
    sum_back(range(6, 9))
    advance(2, 2)
    for copy in give[2]:
        copy.start()
    forward(1, 2)
    forward(2, 3)
    advance(3, 1)
    advance(4, 0)
    forward(3, 4)
    advance(3, 2)
    advance(4, 1)
    for c in range(NC):
        rows = pl.ds(c * A, A)
        total = nt(oh_t[...], yT[pl.ds(c * C, C), :])
        upd[rows, :] = (coef[rows, :].astype(F32) + total).astype(BF16)
    stores[6].start()
    advance(4, 2)
    advance(5, 0)
    for pair in give:
        for copy in pair:
            copy.wait_recv()
    gco[...] = (
        (cot[...].astype(F32) + own_sum[...]) + (RB[0].astype(F32) + RB[1].astype(F32))
    ).astype(BF16)
    stores[7].start()
    advance(5, 1)
    advance(5, 2)
    for p in range(3):
        for copy in share[p]:
            copy.wait_recv()
        stores[3 + p].start()
    for group in (*halo, *give, swap, *share, *(part for stage in stages for part in stage)):
        for copy in group:
            copy.wait_send()
    for copy in stores:
        copy.wait()


RUNS = ((0, 3, 0, 0), (3, 3, 0, 1), (6, 4, 1, 0), (10, 3, 0, 2), (13, 4, 1, 1), (17, 2, 2, 0))


def finish(upd, gco, O, upd_out, gco_out, g_zero, g_one, g_two, near, rows_near, zero, one, two, sem):
    count = len(RUNS)
    through = [
        [
            pltpu.make_async_copy(start, rows_near.at[i], sem.at[3 * count + 2 * i]),
            pltpu.make_async_copy(rows_near.at[i], end, sem.at[3 * count + 2 * i + 1]),
        ]
        for i, (start, end) in enumerate(((upd, upd_out), (gco, gco_out)))
    ]
    reads = []
    for i, (t, n, _, _) in enumerate(RUNS):
        rows = pl.ds(t * C, n * C)
        reads.append(pltpu.make_async_copy(O.at[:, rows], near.at[:, rows], sem.at[i]))
    for copy in reads + [inward for inward, _ in through]:
        copy.start()
    writes = []
    for i, (t, n, kind, row) in enumerate(RUNS):
        reads[i].wait()
        rows = pl.ds(row * C, C)
        parts = ((zero, g_zero),) if kind == 0 else ((one, g_one), (two, g_two))[kind - 1 : kind]
        held, far = parts[0]
        for part in range(1 if kind == 0 else 2):
            block = held if kind == 0 else held.at[part]
            width = n if kind == 0 else n // 2
            for j in range(width):
                for k in range(2):
                    block[rows, pl.ds(j * C + k * 128, 128)] = near[
                        k, pl.ds((t + part * width + j) * C, C), :
                    ].astype(F32)
            write = pltpu.make_async_copy(
                block.at[rows],
                (far if kind == 0 else far.at[part]).at[rows],
                sem.at[count + 2 * i + part],
            )
            write.start()
            writes.append(write)
    for inward, outward in through:
        inward.wait()
        outward.start()
        writes.append(outward)
    for copy in writes:
        copy.wait()


def vmem(*shape):
    return pltpu.VMEM(shape, BF16)


def work(coef, cot, w0, w1, w2, rot, src, tgt, gate, live):
    whole = pl.BlockSpec(memory_space=pltpu.VMEM)
    far = pl.BlockSpec(memory_space=pltpu.HBM)
    return pl.pallas_call(
        body,
        out_shape=(
            jax.ShapeDtypeStruct((NC * A, C), BF16),
            jax.ShapeDtypeStruct((NC * A, C), BF16),
            jax.ShapeDtypeStruct((ROWS, 128), BF16),
        ),
        in_specs=[far] * 6 + [whole] * 3 + [pl.BlockSpec(memory_space=pltpu.SMEM)],
        out_specs=(far,) * 3,
        scratch_shapes=[
            vmem(NC * A, C),
            vmem(NC * A, C),
            vmem(ROT, E),
            vmem(NC * A, C),
            vmem(NC * A, C),
            vmem(ROWS, 128),
            vmem(768, 768),
            vmem(2, 512, 512),
            vmem(2, 256, 256),
            vmem(W9, E),
            vmem(W9, E),
            vmem(W9, E),
            pltpu.VMEM((W9, EB), F32),
            pltpu.VMEM((NC * A, C), F32),
            vmem(2, NC * A, C),
            vmem(W9, 3 * A),
            vmem(W9, A),
            vmem(768, 768),
            vmem(1024, 1024),
            vmem(1024, 1024),
            vmem(512, 512),
            vmem(512, 512),
            pltpu.VMEM((ROT, 8, E), F32),
            vmem(3 * A, E),
            vmem(A, E),
            vmem(ROWS, 128),
            vmem(HALF, 128),
            vmem(HALF, 128),
            vmem(3, HALF // 4, 128),
            pltpu.VMEM((HALF // 4, 128), F32),
            pltpu.VMEM((3, HALF // 16, 128), F32),
            pltpu.VMEM((HALF // 16, 128), F32),
            pltpu.VMEM((3, HALF // 16, 128), F32),
            vmem(2, NC * A, C),
            vmem(2, NC * A, C),
            pltpu.SemaphoreType.DMA((2, 5)),
            pltpu.SemaphoreType.DMA((2, 5)),
            pltpu.SemaphoreType.DMA((5, 3)),
            pltpu.SemaphoreType.DMA((5, 3)),
            pltpu.SemaphoreType.DMA((5, 3, 3)),
            pltpu.SemaphoreType.DMA((5, 3, 3)),
            pltpu.SemaphoreType.DMA((6,)),
            pltpu.SemaphoreType.DMA((8,)),
        ],
        compiler_params=pltpu.CompilerParams(
            collective_id=0, has_side_effects=True, vmem_limit_bytes=56 * 2**20
        ),
        name="layer",
    )(coef, cot, w0, w1, w2, rot, src, tgt, gate, live)


def shards(coeffs, cotangent, w_zero, w_one, w_two, source, target, rotation, gate, tile_live):
    def by_coef(rows):
        return jnp.transpose(rows[0], (1, 0, 2)).reshape(NC * A, C)

    def by_atom(rows):
        return jnp.transpose(rows.reshape(NC, A, C), (1, 0, 2))[None]

    upd, gco, grads = work(
        by_coef(coeffs), by_coef(cotangent), w_zero, w_one, w_two,
        rotation[0], source, target, gate, tile_live,
    )
    far = pl.BlockSpec(memory_space=pltpu.HBM)
    upd, gco, zero, one, two = pl.pallas_call(
        finish,
        out_shape=(
            jax.ShapeDtypeStruct((NC * A, C), BF16),
            jax.ShapeDtypeStruct((NC * A, C), BF16),
            jax.ShapeDtypeStruct((768, 768), F32),
            jax.ShapeDtypeStruct((2, 512, 512), F32),
            jax.ShapeDtypeStruct((2, 256, 256), F32),
        ),
        in_specs=[far] * 3,
        out_specs=(far,) * 5,
        scratch_shapes=[
            vmem(2, HALF, 128),
            vmem(2, NC * A, C),
            pltpu.VMEM((768, 768), F32),
            pltpu.VMEM((2, 512, 512), F32),
            pltpu.VMEM((2, 256, 256), F32),
            pltpu.SemaphoreType.DMA((3 * len(RUNS) + 4,)),
        ],
        compiler_params=pltpu.CompilerParams(vmem_limit_bytes=62 * 2**20),
        name="finish",
    )(upd, gco, grads.reshape(2, HALF, 128))
    return by_atom(upd), by_atom(gco), zero, one, two


def solution(mesh):
    return jax.shard_map(
        shards,
        mesh=mesh,
        in_specs=(
            P("dp", "help", None, None),
            P("dp", "help", None, None),
            P(),
            P(),
            P(),
            P("dp", "help"),
            P("dp", "help"),
            P("dp", None, "help"),
            P("dp", "help"),
            P("dp", "help"),
        ),
        out_specs=(P("dp", "help", None, None), P("dp", "help", None, None), P(), P(), P()),
        check_vma=False,
    )
```
